32 devices in a mesh: groups: 1, row: 32 (over z, y, x, core).
Axes of the slice: x: 2, y: 2, z: 4, core: 2. Of those that a mesh axis runs over, the one named last changes fastest.
Arguments:
- pair: float32 [384, 384, 128], P(('groups', 'row')), may hold values from -6 to 6
- mask: int32 [384], P('groups'), may hold values from 0 to 1, as said below
- tri_in: bfloat16 [128, 512], replicated, may hold values from -0.5 to 0.5
- tri_gate: bfloat16 [128, 128], replicated, may hold values from -0.5 to 0.5
- tri_out: bfloat16 [128, 128], replicated, may hold values from -0.5 to 0.5
- att_in: bfloat16 [128, 512], replicated
- att_bias: bfloat16 [128, 4], replicated, may hold values from -0.5 to 0.5
- att_out: bfloat16 [128, 128], replicated, may hold values from -0.5 to 0.5
Outputs:
- updated: float32 [384, 384, 128], P(('groups', 'row'))
The draws below stay inside these ranges and needn't reach their ends.
Inputs may be any that keep to these rules, and one draw needn't show every extreme that they name: mask is 1 on the first L residues and 0 on the rest, with 192 <= L < 384.
All inputs are finite; a program needn't handle non-finite values.
Results may differ from the reference program's by a relative error of at most 0.0075.
Values may be sent and summed in bfloat16 or wider, within the bound.
A program may use at most 192 MiB of HBM per device.

```python
import jax
import jax.numpy as jnp
from jax import lax

C = 128
HEADS = 4
HEAD = 32
RES = 384
HD = 128


def draw_mask(key, part):
    key = jax.random.fold_in(key, 3)
    length = jax.random.randint(key, (), RES // 2, RES)
    return (jnp.arange(RES) < length).astype(jnp.int32)


def draw_att_in(key, part):
    key = jax.random.fold_in(key, 7)
    base = jax.random.normal(key, (C, 4 * HD), jnp.float32) * C ** (-0.5)
    return base.astype(jnp.bfloat16)


def shard_levels(key, extent, split, least, top_value):
    loudness, own = 1.0, jax.random.fold_in(key, 6)
    for dim, shards_of in split:
        steps = jnp.exp(jax.random.uniform(jax.random.fold_in(own, dim), (shards_of,), jnp.float32, least / len(split), top_value / len(split)))
        loudness = loudness * jnp.repeat(steps, extent[dim] // shards_of).reshape([-1 if axis == dim else 1 for axis in range(len(extent))])
    return loudness


def normal_values(own_key, shape, deviation, most, pieces=(), kind=jnp.bfloat16):
    result = deviation * jax.random.normal(own_key, shape, jnp.float32)
    if pieces:
        result = result * shard_levels(own_key, shape, pieces, -0.22, 0.18)
    return jnp.clip(result, -most, most).astype(kind)


def setup_inputs(seed: int = 0, part: int = 0) -> dict:
    key_of = jax.random.split(jax.random.key(seed), 9)
    own_keys = jax.random.split(jax.random.fold_in(key_of[8], part), 9)
    return {
        "pair": normal_values(own_keys[0], (RES, RES, C), 1.0, 6.0, ((0, 32),), jnp.float32),
        "mask": draw_mask(jax.random.fold_in(jax.random.fold_in(key_of[8], part), 71), part),
        "tri_in": normal_values(key_of[2], (C, 4 * C), C ** -0.5, 0.5),
        "tri_gate": normal_values(key_of[3], (C, C), C ** -0.5, 0.5),
        "tri_out": normal_values(key_of[4], (C, C), C ** -0.5, 0.5),
        "att_in": draw_att_in(jax.random.fold_in(key_of[8], 71), part),
        "att_bias": normal_values(key_of[6], (C, HEADS), C ** -0.5, 0.5),
        "att_out": normal_values(key_of[7], (HD, C), HD ** -0.5, 0.5),
    }


def layer_norm(value):
    center = value - lax.optimization_barrier(jnp.mean(value, axis=-1, keepdims=True))
    return center / jnp.sqrt(lax.optimization_barrier(jnp.mean(center * center, axis=-1, keepdims=True)) + 1e-05)

def reference(pair, mask, tri_in, tri_gate, tri_out, att_in, att_bias, att_out):
    valid = mask.astype(jnp.float32)
    pair_mask = valid[:, None] * valid[None, :]
    normed = layer_norm(pair).astype(jnp.bfloat16)
    flat = normed.reshape(RES * RES, C)
    proj = jnp.dot(flat, tri_in, preferred_element_type=jnp.float32).reshape(RES, RES, 4 * C)
    left = (jax.nn.sigmoid(proj[..., C:2 * C]) * proj[..., :C] * pair_mask[..., None]).astype(jnp.bfloat16)
    right = (jax.nn.sigmoid(proj[..., 3 * C:]) * proj[..., 2 * C:3 * C] * pair_mask[..., None]).astype(jnp.bfloat16)
    tri = jnp.einsum('ikc,jkc->ijc', left.astype(jnp.float32), right.astype(jnp.float32))
    tnorm = layer_norm(tri).astype(jnp.bfloat16).reshape(RES * RES, C)
    update = jnp.dot(tnorm, tri_out, preferred_element_type=jnp.float32)
    gating = jax.nn.sigmoid(jnp.dot(flat, tri_gate, preferred_element_type=jnp.float32))
    pair1 = pair + pair_mask[..., None] * (gating * update).reshape(RES, RES, C)
    ynorm = layer_norm(pair1).astype(jnp.bfloat16).reshape(RES * RES, C)
    qkvg = jnp.dot(ynorm, att_in, preferred_element_type=jnp.float32).reshape(RES, RES, 4, HEADS, HEAD)
    query = qkvg[:, :, 0].astype(jnp.bfloat16)
    keys = qkvg[:, :, 1].astype(jnp.bfloat16)
    values = qkvg[:, :, 2].astype(jnp.bfloat16)
    gates = qkvg[:, :, 3]
    bias = jnp.dot(ynorm, att_bias, preferred_element_type=jnp.float32).astype(jnp.bfloat16)
    bias = jnp.transpose(bias.reshape(RES, RES, HEADS), (2, 0, 1)).astype(jnp.float32)

    def one_row(inputs):
        q_row, k_row, v_row, g_row = inputs
        scores = jnp.einsum('jhd,khd->hjk', q_row.astype(jnp.float32), k_row.astype(jnp.float32)) / jnp.sqrt(jnp.float32(HEAD)) + bias
        scores = jnp.where(mask[None, None, :] > 0, scores, jnp.float32(-1000000000.0))
        probs = jax.nn.softmax(scores, axis=-1).astype(jnp.bfloat16)
        mixed = jnp.einsum('hjk,khd->jhd', probs.astype(jnp.float32), v_row.astype(jnp.float32))
        return (jax.nn.sigmoid(g_row) * mixed).astype(jnp.bfloat16).reshape(RES, HD)
    att = lax.map(one_row, (query, keys, values, gates))
    out = jnp.dot(att.reshape(RES * RES, HD), att_out, preferred_element_type=jnp.float32).reshape(RES, RES, C)
    return pair1 + valid[:, None, None] * out
```

```python
import functools
import math

import jax
import jax.numpy as jnp
from jax import lax
from jax.experimental import pallas as pl
from jax.experimental.pallas import tpu as pltpu
from jax.sharding import PartitionSpec as P

EPS = 1e-05
LOG2E = math.log2(math.e)
MESH = pl.DeviceIdType.MESH
PLANE = 8


def sigmoid(value):
    return 0.5 * jnp.tanh(0.5 * value) + 0.5


def norm_rows(value):
    center = value - jnp.mean(value, axis=0, keepdims=True)
    return center * lax.rsqrt(jnp.mean(center * center, axis=0, keepdims=True) + EPS)


def scatter_rows(ref, first, stride, value):
    for q in range(ref.shape[0]):
        ref[q, pl.ds(first, value.shape[0], stride=stride), :] = value[:, q * 128 : (q + 1) * 128]


def gather_rows(ref, first, count, stride):
    parts = [ref[q, pl.ds(first, count, stride=stride), :] for q in range(ref.shape[0])]
    return jnp.concatenate(parts, axis=1)


def all_rows(ref):
    return jnp.concatenate([ref[q] for q in range(ref.shape[0])], axis=1)


def matmul(a, b):
    return jnp.dot(a, b, preferred_element_type=jnp.float32)


def triangle_kernel(
    n, pair_ref, pm_ref, tri_in_ref, gate_ref, tri_out_ref, bias_w_ref,
    pair1_ref, yn_ref, bias_ref,
    wide, square, xn, left_send, right_send, left_got, right_got, left_mat, tri_send, tri_got, bias_all, bias_wide,
    left_ssem, left_rsem, right_ssem, right_rsem, tri_ssem, tri_rsem,
    z_ssem, plane_ssem, core_ssem, bias_rsem,
):
    rows, residues, width = pair_ref.shape
    per = width // n
    block = per * rows
    heads = bias_w_ref.shape[0]
    me = lax.axis_index("row")
    group = lax.axis_index("groups")

    def peer(t):
        return lax.rem(me + (t % 2) * (n // 2) + t // 2, n)

    def copy_to(src, dst, ssem, rsem, device):
        return pltpu.make_async_remote_copy(
            src_ref=src, dst_ref=dst, send_sem=ssem, recv_sem=rsem,
            device_id=(group, device), device_id_type=MESH,
        )

    def exchange_start(send, got, ssem, rsem):
        def body(t, _):
            d = peer(t)
            copy_to(send.at[d], got.at[me], ssem.at[d], rsem.at[me], d).start()
            return 0
        lax.fori_loop(1, n, body, 0)

    def exchange_recv(send, got, ssem, rsem):
        def body(t, _):
            s = lax.rem(me + t, n)
            copy_to(send.at[s], got.at[s], ssem.at[s], rsem.at[s], s).wait_recv()
            return 0
        lax.fori_loop(1, n, body, 0)

    def exchange_sent(send, got, ssem, rsem):
        def body(t, _):
            d = lax.rem(me + t, n)
            copy_to(send.at[d], got.at[me], ssem.at[d], rsem.at[me], d).wait_send()
            return 0
        lax.fori_loop(1, n, body, 0)

    barrier = pltpu.get_barrier_semaphore()

    def greet(t, _):
        pl.semaphore_signal(barrier, inc=1, device_id=(group, lax.rem(me + t, n)), device_id_type=MESH)
        return 0
    lax.fori_loop(1, n, greet, 0)

    def narrow(dst):
        def body(d, _):
            for q in range(wide.shape[0]):
                part = wide[q, pl.ds(pl.multiple_of(d * block, 16), block), :]
                dst[d, :, q * 128 : (q + 1) * 128] = part.astype(jnp.bfloat16)
            return 0
        lax.fori_loop(0, n, body, 0)

    def widen(src):
        def body(d, _):
            for q in range(wide.shape[0]):
                part = src[d, :, q * 128 : (q + 1) * 128].astype(jnp.float32)
                wide[q, pl.ds(pl.multiple_of(d * block, 16), block), :] = part
            return 0
        lax.fori_loop(0, n, body, 0)

    def gated(r, first, normed):
        proj = matmul(tri_in_ref[first : first + 2 * width, :], normed)
        value = sigmoid(proj[width:]) * proj[:width] * pm_ref[r]
        scatter_rows(wide, r, rows, value)

    def left_row(r, _):
        normed = norm_rows(pair_ref[r].T).astype(jnp.bfloat16)
        xn[r] = normed
        gated(r, 0, normed)
        return 0
    lax.fori_loop(0, rows, left_row, 0)
    narrow(left_send)
    pl.semaphore_wait(barrier, n - 1)
    exchange_start(left_send, left_got, left_ssem, left_rsem)

    def right_row(r, _):
        gated(r, 2 * width, xn[r])
        return 0
    lax.fori_loop(0, rows, right_row, 0)
    narrow(right_send)
    exchange_start(right_send, right_got, right_ssem, right_rsem)

    left_got[me] = left_send[me]
    right_got[me] = right_send[me]
    exchange_recv(left_send, left_got, left_ssem, left_rsem)
    widen(left_got)
    for c in range(per):
        for r in range(rows):
            left_mat[c, r * n : (r + 1) * n, :] = gather_rows(wide, c * rows + r, n, block).astype(jnp.bfloat16)
    exchange_recv(right_send, right_got, right_ssem, right_rsem)
    widen(right_got)
    for c in range(per):
        for r in range(rows):
            scatter_rows(square.at[c], r, rows, gather_rows(wide, c * rows + r, n, block))
    for c in range(per):
        tri = lax.dot_general(
            left_mat[c], all_rows(square.at[c]).astype(jnp.bfloat16), (((1,), (1,)), ((), ())),
            preferred_element_type=jnp.float32,
        )
        for r in range(rows):
            scatter_rows(wide, c * rows + r, block, tri[r * n : (r + 1) * n])
    narrow(tri_send)
    exchange_start(tri_send, tri_got, tri_ssem, tri_rsem)
    tri_got[me] = tri_send[me]
    exchange_recv(tri_send, tri_got, tri_ssem, tri_rsem)
    widen(tri_got)

    def pair_row(r, _):
        tnorm = norm_rows(gather_rows(wide, r, width, rows)).astype(jnp.bfloat16)
        update = matmul(tri_out_ref[...], tnorm)
        gating = sigmoid(matmul(gate_ref[...], xn[r]))
        pair1 = pair_ref[r].T + pm_ref[r] * (gating * update)
        pair1_ref[r] = pair1
        yn = norm_rows(pair1).astype(jnp.bfloat16)
        yn_ref[r] = yn
        scatter_rows(bias_wide, r, rows, matmul(bias_w_ref[...], yn))
        return 0
    lax.fori_loop(0, rows, pair_row, 0)
    bias_all[me] = all_rows(bias_wide).astype(jnp.bfloat16)

    planes = n // PLANE
    low = lax.rem(me, PLANE)
    core = lax.rem(me, 2)
    base = me - low
    other = base + low - core + (1 - core)

    def put(b, ssem, device):
        return copy_to(bias_all.at[b], bias_all.at[b], ssem, bias_rsem.at[b], device)

    def along(step):
        return lax.rem(me + step * PLANE, n)

    def beside(step):
        return base + lax.rem(low + 2 * step, PLANE)

    for step in range(1, planes):
        put(me, z_ssem.at[step], along(step)).start()
    for z in range(planes):
        b = along(z)
        if z:
            put(b, z_ssem.at[z], me).wait_recv()
        for step in range(1, PLANE // 2):
            put(b, plane_ssem.at[z, step], beside(step)).start()
        put(b, core_ssem.at[z, 0], other).start()
    for z in range(planes):
        for step in range(1, PLANE // 2):
            b = lax.rem(beside(step) + z * PLANE, n)
            put(b, plane_ssem.at[z, step], me).wait_recv()
            put(b, core_ssem.at[z, step], other).start()
    for z in range(planes):
        for step in range(PLANE // 2):
            b = lax.rem(base + lax.rem(low - core + (1 - core) + 2 * step, PLANE) + z * PLANE, n)
            put(b, core_ssem.at[z, step], me).wait_recv()
    for step in range(1, planes):
        put(me, z_ssem.at[step], along(step)).wait_send()
    for z in range(planes):
        for step in range(PLANE // 2):
            b = lax.rem(beside(step) + z * PLANE, n)
            put(b, core_ssem.at[z, step], other).wait_send()
            if step:
                put(b, plane_ssem.at[z, step], beside(step)).wait_send()
    bias_ref[...] = bias_all[...]
    exchange_sent(left_send, left_got, left_ssem, left_rsem)
    exchange_sent(right_send, right_got, right_ssem, right_rsem)
    exchange_sent(tri_send, tri_got, tri_ssem, tri_rsem)


def attention_kernel(rows, heads, bias_ref, hide_ref, pair1_ref, yn_ref, live_ref, att_in_ref, att_out_ref, out_ref, wide, square, bias_t):
    n, block, residues = bias_ref.shape
    width = yn_ref.shape[1]
    hd = att_out_ref.shape[1]
    size = hd // heads

    @pl.when(pl.program_id(0) == 0)
    def _():
        for d in range(n):
            for q in range(wide.shape[0]):
                part = bias_ref[d, :, q * 128 : (q + 1) * 128].astype(jnp.float32)
                wide[q, d * block : (d + 1) * block, :] = part * LOG2E
        for h in range(heads):
            for r in range(rows):
                scatter_rows(square, r, rows, gather_rows(wide, h * rows + r, n, block))
            bias_t[h] = (all_rows(square) + hide_ref[...]).T

    qkvg = matmul(att_in_ref[...], yn_ref[0])
    query = (qkvg[:hd] * (LOG2E / math.sqrt(size))).astype(jnp.bfloat16)
    keys = qkvg[hd : 2 * hd].astype(jnp.bfloat16)
    values = qkvg[2 * hd : 3 * hd].astype(jnp.bfloat16)
    gates = sigmoid(qkvg[3 * hd :])
    ones = jnp.ones((16, residues), jnp.bfloat16)
    parts = []
    for h in range(heads):
        at = slice(h * size, (h + 1) * size)
        scores = lax.dot_general(keys[at], query[at], (((0,), (0,)), ((), ())), preferred_element_type=jnp.float32)
        scores = scores + bias_t[h]
        probs = jnp.exp2(scores - jnp.max(scores, axis=0, keepdims=True)).astype(jnp.bfloat16)
        mixed = matmul(jnp.concatenate([values[at], ones], axis=0), probs)
        parts.append((mixed[:size] * (1.0 / mixed[size : size + 1]) * gates[at]).astype(jnp.bfloat16))
    att = jnp.concatenate(parts, axis=0)
    out = matmul(att_out_ref[...], att)
    out_ref[0] = (pair1_ref[0] + live_ref[0] * out).T


def fused(n, pair, mask, tri_in, tri_gate, tri_out, att_in, att_bias, att_out):
    rows, residues, width = pair.shape
    heads = att_bias.shape[1]
    hd = att_out.shape[0]
    per = width // n
    block = per * rows
    valid = mask.astype(jnp.float32)
    row_valid = lax.dynamic_slice_in_dim(valid, lax.axis_index("row") * rows, rows, 0)
    live = jnp.broadcast_to(row_valid[:, None, None], (rows, 1, residues))
    pm = live * valid[None, None, :]
    hide = jnp.where(mask > 0, 0.0, -jnp.inf).astype(jnp.float32)[None, :]
    bf, f32 = jnp.bfloat16, jnp.float32
    vmem = pl.BlockSpec(memory_space=pltpu.VMEM)
    dma = pltpu.SemaphoreType.DMA
    blocks = pltpu.VMEM((n, block, residues), bf)
    planes = n // PLANE
    pair1, yn, bias = pl.pallas_call(
        functools.partial(triangle_kernel, n),
        out_shape=(
            jax.ShapeDtypeStruct((rows, width, residues), f32),
            jax.ShapeDtypeStruct((rows, width, residues), bf),
            jax.ShapeDtypeStruct((n, heads * rows, residues), bf),
        ),
        in_specs=[vmem] * 6,
        out_specs=(vmem, vmem, vmem),
        scratch_shapes=[
            pltpu.VMEM((residues // 128, n * block, 128), f32),
            pltpu.VMEM((per, residues // 128, residues, 128), f32),
            pltpu.VMEM((rows, width, residues), bf),
            blocks, blocks, blocks, blocks,
            pltpu.VMEM((per, residues, residues), bf),
            blocks, blocks,
            pltpu.VMEM((n, heads * rows, residues), bf),
            pltpu.VMEM((residues // 128, heads * rows, 128), f32),
        ] + [dma((n,))] * 6 + [
            dma((planes,)), dma((planes, PLANE // 2)), dma((planes, PLANE // 2)), dma((n,)),
        ],
        compiler_params=pltpu.CompilerParams(
            collective_id=0, has_side_effects=True, vmem_limit_bytes=48 * 2**20
        ),
    )(pair, pm, tri_in.T, tri_gate.T, tri_out.T, att_bias.T)

    def whole(shape):
        return pl.BlockSpec(shape, lambda i: (0,) * len(shape))

    def row(*shape):
        return pl.BlockSpec((1,) + shape, lambda i: (i, 0, 0))

    return pl.pallas_call(
        functools.partial(attention_kernel, rows, heads),
        grid=(rows,),
        out_shape=jax.ShapeDtypeStruct((rows, residues, width), f32),
        in_specs=[
            whole((n, heads * rows, residues)), whole((1, residues)), row(width, residues), row(width, residues),
            row(1, residues), whole((4 * hd, width)), whole((width, hd)),
        ],
        out_specs=row(residues, width),
        scratch_shapes=[
            pltpu.VMEM((residues // 128, n * heads * rows, 128), f32),
            pltpu.VMEM((residues // 128, residues, 128), f32),
            pltpu.VMEM((heads, residues, residues), f32),
        ],
        compiler_params=pltpu.CompilerParams(vmem_limit_bytes=48 * 2**20),
    )(bias, hide, pair1, yn, live, att_in.T, att_out.T)


def layer_norm(value):
    center = value - jnp.mean(value, axis=-1, keepdims=True)
    return center / jnp.sqrt(jnp.mean(center * center, axis=-1, keepdims=True) + 1e-05)


def per_device(pair, mask, tri_in, tri_gate, tri_out, att_in, att_bias, att_out):
    own_rows = pair.shape[0]
    residues = pair.shape[1]
    width = pair.shape[2]
    heads = att_bias.shape[1]
    head_size = att_out.shape[0] // heads
    valid = mask.astype(jnp.float32)
    start_row = lax.axis_index("row") * own_rows
    row_valid = lax.dynamic_slice_in_dim(valid, start_row, own_rows, 0)
    pair_mask = row_valid[:, None] * valid[None, :]
    normed = layer_norm(pair).astype(jnp.bfloat16)
    proj = jnp.einsum("rkc,cf->rkf", normed, tri_in, preferred_element_type=jnp.float32)
    left = (
        jax.nn.sigmoid(proj[..., width : 2 * width]) * proj[..., :width] * pair_mask[..., None]
    ).astype(jnp.bfloat16)
    right = (
        jax.nn.sigmoid(proj[..., 3 * width :])
        * proj[..., 2 * width : 3 * width]
        * pair_mask[..., None]
    ).astype(jnp.bfloat16)
    left_by_channel = jnp.transpose(left, (2, 0, 1))
    right_by_channel = jnp.transpose(right, (2, 0, 1))
    left_all, right_all = (
        lax.all_to_all(left_by_channel, "row", split_axis=0, concat_axis=1, tiled=True),
        lax.all_to_all(right_by_channel, "row", split_axis=0, concat_axis=1, tiled=True),
    )
    tri_channel = jnp.einsum(
        "cik,cjk->cij", left_all, right_all, preferred_element_type=jnp.float32
    )
    tri_rows = lax.all_to_all(
        tri_channel.astype(jnp.bfloat16), "row", split_axis=1, concat_axis=0, tiled=True
    ).astype(tri_channel.dtype)
    tri = jnp.transpose(tri_rows, (1, 2, 0))
    tnorm = layer_norm(tri).astype(jnp.bfloat16)
    update = jnp.einsum("rkc,cf->rkf", tnorm, tri_out, preferred_element_type=jnp.float32)
    gating = jax.nn.sigmoid(
        jnp.einsum("rkc,cf->rkf", normed, tri_gate, preferred_element_type=jnp.float32)
    )
    pair1 = pair + pair_mask[..., None] * gating * update
    ynorm = layer_norm(pair1).astype(jnp.bfloat16)
    qkvg = jnp.einsum("rkc,cf->rkf", ynorm, att_in, preferred_element_type=jnp.float32)
    qkvg = qkvg.reshape(own_rows, residues, 4, heads, head_size)
    query = qkvg[:, :, 0].astype(jnp.bfloat16)
    keys = qkvg[:, :, 1].astype(jnp.bfloat16)
    values = qkvg[:, :, 2].astype(jnp.bfloat16)
    gates = qkvg[:, :, 3]
    local_bias = jnp.einsum(
        "rkc,ch->hrk", ynorm, att_bias, preferred_element_type=jnp.float32
    ).astype(jnp.bfloat16)
    bias = lax.all_gather(local_bias, "row", axis=1, tiled=True)
    scores = jnp.einsum(
        "ijhd,ikhd->ihjk", query, keys, preferred_element_type=jnp.float32
    ) / jnp.sqrt(jnp.float32(head_size))
    scores = scores + bias.astype(jnp.float32)[None]
    scores = jnp.where(mask[None, None, None, :] > 0, scores, jnp.float32(-1000000000.0))
    probs = jax.nn.softmax(scores, axis=-1).astype(jnp.bfloat16)
    mixed = jnp.einsum("ihjk,ikhd->ijhd", probs, values, preferred_element_type=jnp.float32)
    att = (
        (jax.nn.sigmoid(gates) * mixed)
        .astype(jnp.bfloat16)
        .reshape(own_rows, residues, heads * head_size)
    )
    out = jnp.einsum("rkf,fc->rkc", att, att_out, preferred_element_type=jnp.float32)
    return pair1 + row_valid[:, None, None] * out


def solution(mesh):
    n = mesh.shape["row"]

    def per_shard(pair, mask, tri_in, tri_gate, tri_out, att_in, att_bias, att_out):
        rows, residues, width = pair.shape
        fits = (
            width % n == 0 and n % 16 == 0 and n % PLANE == 0 and residues % 128 == 0
            and (width // n * rows) % 16 == 0 and (att_bias.shape[1] * rows) % 16 == 0
        )
        run = functools.partial(fused, n) if fits else per_device
        return run(pair, mask, tri_in, tri_gate, tri_out, att_in, att_bias, att_out)

    return jax.shard_map(
        per_shard,
        mesh=mesh,
        in_specs=(P(("groups", "row"), None, None), P("groups"), P(), P(), P(), P(), P(), P()),
        out_specs=P(("groups", "row"), None, None),
        check_vma=False,
    )
```

```python
import functools
import math

import jax
import jax.numpy as jnp
from jax import lax
from jax.experimental import pallas as pl
from jax.experimental.pallas import tpu as pltpu
from jax.sharding import PartitionSpec as P

EPS = 1e-05
LOG2E = math.log2(math.e)
MESH = pl.DeviceIdType.MESH
PLANE = 8


def sigmoid(value):
    return 0.5 * jnp.tanh(0.5 * value) + 0.5


def norm_rows(value):
    center = value - jnp.mean(value, axis=0, keepdims=True)
    return center * lax.rsqrt(jnp.mean(center * center, axis=0, keepdims=True) + EPS)


def scatter_rows(ref, first, stride, value):
    for q in range(ref.shape[0]):
        ref[q, pl.ds(first, value.shape[0], stride=stride), :] = value[:, q * 128 : (q + 1) * 128]


def gather_rows(ref, first, count, stride):
    parts = [ref[q, pl.ds(first, count, stride=stride), :] for q in range(ref.shape[0])]
    return jnp.concatenate(parts, axis=1)


def all_rows(ref):
    return jnp.concatenate([ref[q] for q in range(ref.shape[0])], axis=1)


def matmul(a, b):
    return jnp.dot(a, b, preferred_element_type=jnp.float32)


def to_t(ref):
    return ref[...].astype(jnp.float32).T.astype(jnp.bfloat16)


def triangle_kernel(
    n, chunk, heads,
    pair_ref, mask_ref, live_ref, tri_in_ref, gate_ref, tri_out_ref, att_in_ref, bias_w_ref,
    pair1_ref, qkv_ref, g_ref, bias_ref,
    wide, bias_wide, square, right_mat, xn, yn, gating, tri_in_t, gate_t, tri_out_t, att_in_t,
    left_send, right_send, tri_send, left_got, right_got, tri_got, bias_all,
    left_ssem, left_rsem, right_ssem, right_rsem, tri_ssem, tri_rsem,
    z_ssem, plane_ssem, core_ssem, bias_rsem,
):
    rows, residues, width = pair_ref.shape
    per = width // n
    block = per * chunk
    chunks = rows // chunk
    hd = g_ref.shape[1]
    tiles = residues // 128
    me = lax.axis_index("row")
    group = lax.axis_index("groups")

    def loop(low, high, body):
        def step(i, _):
            body(i)
            return 0
        lax.fori_loop(low, high, step, 0)

    def peer(t):
        return lax.rem(me + (t % 2) * (n // 2) + t // 2, n)

    def copy_to(src, dst, ssem, rsem, device):
        return pltpu.make_async_remote_copy(
            src_ref=src, dst_ref=dst, send_sem=ssem, recv_sem=rsem,
            device_id=(group, device), device_id_type=MESH,
        )

    def outgoing(plan, u, d):
        send, got, ssem, rsem = plan
        return copy_to(send.at[u, d], got.at[u, me], ssem.at[u, d], rsem.at[u, me], d)

    def incoming(plan, u, s):
        send, got, ssem, rsem = plan
        return copy_to(send.at[u, s], got.at[u, s], ssem.at[u, s], rsem.at[u, s], s)

    left = (left_send, left_got, left_ssem, left_rsem)
    right = (right_send, right_got, right_ssem, right_rsem)
    back = (tri_send, tri_got, tri_ssem, tri_rsem)

    def send_chunk(plan, u):
        def narrow(d):
            for q in range(tiles):
                part = wide[q, pl.ds(pl.multiple_of(d * block, 16), block), :]
                plan[0][u, d, :, q * 128 : (q + 1) * 128] = part.astype(jnp.bfloat16)
        loop(0, n, narrow)
        loop(1, n, lambda t: outgoing(plan, u, peer(t)).start())
        plan[1][u, me] = plan[0][u, me]

    def receive_chunk(plan, u):
        loop(1, n, lambda t: incoming(plan, u, lax.rem(me + t, n)).wait_recv())

        def widen(s):
            for q in range(tiles):
                part = plan[1][u, s, :, q * 128 : (q + 1) * 128].astype(jnp.float32)
                wide[q, pl.ds(pl.multiple_of(s * block, 16), block), :] = part
        loop(0, n, widen)

    barrier = pltpu.get_barrier_semaphore()
    loop(1, n, lambda t: pl.semaphore_signal(
        barrier, inc=1, device_id=(group, lax.rem(me + t, n)), device_id_type=MESH))

    valid = mask_ref[...].astype(jnp.float32)

    def pm(r):
        return valid * live_ref[0, me * rows + r].astype(jnp.float32)

    tri_in_t[...] = to_t(tri_in_ref)

    def gated(r, place, first):
        proj = matmul(tri_in_t[first : first + 2 * width, :], xn[r])
        value = sigmoid(proj[width:]) * proj[:width] * pm(r)
        scatter_rows(wide, place, chunk, value)

    for u in range(chunks):
        def right_row(t):
            r = u * chunk + t
            pair_t = pair_ref[r].T
            pair1_ref[r] = pair_t
            xn[r] = norm_rows(pair_t).astype(jnp.bfloat16)
            gated(r, t, 2 * width)
        loop(0, chunk, right_row)
        if u == 0:
            pl.semaphore_wait(barrier, n - 1)
        send_chunk(right, u)
    for u in range(chunks):
        loop(0, chunk, lambda t: gated(u * chunk + t, t, 0))
        send_chunk(left, u)

    gate_t[...] = to_t(gate_ref)
    tri_out_t[...] = to_t(tri_out_ref)
    att_in_t[...] = to_t(att_in_ref)

    def gate_row(r):
        gating[r] = sigmoid(matmul(gate_t[...], xn[r])) * pm(r)
    loop(0, rows, gate_row)

    for u in range(chunks):
        receive_chunk(right, u)
        for c in range(per):
            for t in range(chunk):
                part = gather_rows(wide, c * chunk + t, n, block)
                scatter_rows(square.at[c], u * chunk + t, rows, part)
    for c in range(per):
        right_mat[c] = all_rows(square.at[c]).astype(jnp.bfloat16)
    for u in range(chunks):
        receive_chunk(left, u)
        for c in range(per):
            lefts = [gather_rows(wide, c * chunk + t, n, block) for t in range(chunk)]
            tri = lax.dot_general(
                jnp.concatenate(lefts, axis=0).astype(jnp.bfloat16), right_mat[c],
                (((1,), (1,)), ((), ())), preferred_element_type=jnp.float32,
            )
            for t in range(chunk):
                scatter_rows(wide, c * chunk + t, block, tri[t * n : (t + 1) * n])
        send_chunk(back, u)

    planes = n // PLANE
    low = lax.rem(me, PLANE)
    base = me - low
    twin_low = low - lax.rem(me, 2) + (1 - lax.rem(me, 2))
    twin = base + twin_low

    def put(u, b, ssem, device):
        return copy_to(bias_all.at[u, b], bias_all.at[u, b], ssem, bias_rsem.at[u, b], device)

    def along(step):
        return lax.rem(me + step * PLANE, n)

    def beside(step):
        return base + lax.rem(low + 2 * step, PLANE)

    def bias_first(u):
        for step in range(1, planes):
            put(u, me, z_ssem.at[u, step], along(step)).start()

    def bias_second(u):
        for z in range(planes):
            b = along(z)
            if z:
                put(u, b, z_ssem.at[u, z], me).wait_recv()
            for step in range(1, PLANE // 2):
                put(u, b, plane_ssem.at[u, z, step], beside(step)).start()
            put(u, b, core_ssem.at[u, z, 0], twin).start()

    def bias_third(u):
        for z in range(planes):
            for step in range(1, PLANE // 2):
                b = lax.rem(beside(step) + z * PLANE, n)
                put(u, b, plane_ssem.at[u, z, step], me).wait_recv()
                put(u, b, core_ssem.at[u, z, step], twin).start()

    def bias_last(u):
        for z in range(planes):
            for step in range(PLANE // 2):
                b = lax.rem(base + lax.rem(twin_low + 2 * step, PLANE) + z * PLANE, n)
                put(u, b, core_ssem.at[u, z, step], me).wait_recv()

    def bias_sent(u):
        for step in range(1, planes):
            put(u, me, z_ssem.at[u, step], along(step)).wait_send()
        for z in range(planes):
            for step in range(PLANE // 2):
                b = lax.rem(beside(step) + z * PLANE, n)
                put(u, b, core_ssem.at[u, z, step], twin).wait_send()
                if step:
                    put(u, along(z), plane_ssem.at[u, z, step], beside(step)).wait_send()

    scale = LOG2E / math.sqrt(hd // heads)

    def qkvg_row(r):
        qkvg = matmul(att_in_t[...], yn[r])
        qkv_ref[r, :hd, :] = (qkvg[:hd] * scale).astype(jnp.bfloat16)
        qkv_ref[r, hd:, :] = qkvg[hd : 3 * hd].astype(jnp.bfloat16)
        g_ref[r] = sigmoid(qkvg[3 * hd :])

    for u in range(chunks):
        receive_chunk(back, u)

        def pair_row(t):
            r = u * chunk + t
            tnorm = norm_rows(gather_rows(wide, t, width, chunk)).astype(jnp.bfloat16)
            pair1 = pair1_ref[r] + gating[r] * matmul(tri_out_t[...], tnorm)
            pair1_ref[r] = pair1
            fresh = norm_rows(pair1).astype(jnp.bfloat16)
            yn[r] = fresh
            scatter_rows(bias_wide, t, chunk, matmul(bias_w_ref[...], fresh))
        loop(0, chunk, pair_row)
        bias_all[u, me] = all_rows(bias_wide).astype(jnp.bfloat16)
        bias_first(u)
        if u < chunks - 1:
            loop(u * chunk, (u + 1) * chunk, qkvg_row)
        if u >= 1:
            bias_second(u - 1)
        if u >= 2:
            bias_third(u - 2)
    done = (chunks - 1) * chunk
    half = chunk // 2
    loop(done, done + half, qkvg_row)
    bias_second(chunks - 1)
    if chunks >= 2:
        bias_third(chunks - 2)
    loop(done + half, done + chunk, qkvg_row)
    bias_third(chunks - 1)
    for u in range(chunks):
        bias_last(u)
        bias_ref[u] = bias_all[u]
    for u in range(chunks):
        bias_sent(u)
        for plan in (right, left, back):
            loop(1, n, lambda t: outgoing(plan, u, lax.rem(me + t, n)).wait_send())


def attention_kernel(rows, heads, bias_ref, mask_ref, live_ref, pair1_ref, qkv_ref, g_ref, att_out_ref, out_ref, wide, square, bias_t, out_t):
    chunks, n, block, residues = bias_ref.shape
    hd = g_ref.shape[1]
    size = hd // heads
    chunk = block // heads

    @pl.when(pl.program_id(0) == 0)
    def _():
        out_t[...] = to_t(att_out_ref)
        for u in range(chunks):
            for d in range(n):
                for q in range(wide.shape[0]):
                    part = bias_ref[u, d, :, q * 128 : (q + 1) * 128].astype(jnp.float32)
                    wide[q, d * block : (d + 1) * block, :] = part * LOG2E
            for h in range(heads):
                for t in range(chunk):
                    scatter_rows(square.at[h], u * chunk + t, rows, gather_rows(wide, h * chunk + t, n, block))
        hide = jnp.where(mask_ref[...] > 0, 0.0, -jnp.inf)
        for h in range(heads):
            bias_t[h] = (all_rows(square.at[h]) + hide).T

    ones = jnp.ones((16, residues), jnp.bfloat16)
    parts = []
    for h in range(heads):
        first = h * size
        query = qkv_ref[0, first : first + size, :]
        keys = qkv_ref[0, hd + first : hd + first + size, :]
        values = qkv_ref[0, 2 * hd + first : 2 * hd + first + size, :]
        scores = lax.dot_general(keys, query, (((0,), (0,)), ((), ())), preferred_element_type=jnp.float32)
        scores = scores + bias_t[h]
        probs = jnp.exp2(scores - jnp.max(scores, axis=0, keepdims=True)).astype(jnp.bfloat16)
        mixed = matmul(jnp.concatenate([values, ones], axis=0), probs)
        gates = g_ref[0, first : first + size, :]
        parts.append((mixed[:size] * (1.0 / mixed[size : size + 1]) * gates).astype(jnp.bfloat16))
    out = matmul(out_t[...], jnp.concatenate(parts, axis=0))
    live = live_ref[0, lax.axis_index("row") * rows + pl.program_id(0)].astype(jnp.float32)
    out_ref[0] = (pair1_ref[0] + live * out).T


def chunk_rows(n, rows, width, heads):
    per = width // n
    for chunk in range(1, rows + 1):
        if rows % chunk == 0 and (per * chunk) % 16 == 0 and (heads * chunk) % 16 == 0:
            return chunk
    return 0


def fused(n, pair, mask, tri_in, tri_gate, tri_out, att_in, att_bias, att_out):
    rows, residues, width = pair.shape
    heads = att_bias.shape[1]
    hd = att_out.shape[0]
    per = width // n
    chunk = chunk_rows(n, rows, width, heads)
    chunks = rows // chunk
    tiles = residues // 128
    planes = n // PLANE
    flat = mask.reshape(1, residues)
    bf, f32 = jnp.bfloat16, jnp.float32
    vmem = pl.BlockSpec(memory_space=pltpu.VMEM)
    smem = pl.BlockSpec(memory_space=pltpu.SMEM)
    dma = pltpu.SemaphoreType.DMA
    blocks = pltpu.VMEM((chunks, n, per * chunk, residues), bf)
    side = PLANE // 2
    pair1, qkv, gates, bias = pl.pallas_call(
        functools.partial(triangle_kernel, n, chunk, heads),
        out_shape=(
            jax.ShapeDtypeStruct((rows, width, residues), f32),
            jax.ShapeDtypeStruct((rows, 3 * hd, residues), bf),
            jax.ShapeDtypeStruct((rows, hd, residues), f32),
            jax.ShapeDtypeStruct((chunks, n, heads * chunk, residues), bf),
        ),
        in_specs=[vmem, vmem, smem] + [vmem] * 5,
        out_specs=(vmem,) * 4,
        scratch_shapes=[
            pltpu.VMEM((tiles, width * chunk, 128), f32),
            pltpu.VMEM((tiles, heads * chunk, 128), f32),
            pltpu.VMEM((per, tiles, residues, 128), f32),
            pltpu.VMEM((per, residues, residues), bf),
            pltpu.VMEM((rows, width, residues), bf),
            pltpu.VMEM((rows, width, residues), bf),
            pltpu.VMEM((rows, width, residues), f32),
            pltpu.VMEM((4 * width, width), bf),
            pltpu.VMEM((width, width), bf),
            pltpu.VMEM((width, width), bf),
            pltpu.VMEM((4 * hd, width), bf),
        ] + [blocks] * 6 + [
            pltpu.VMEM((chunks, n, heads * chunk, residues), bf),
        ] + [dma((chunks, n))] * 6 + [
            dma((chunks, planes)), dma((chunks, planes, side)), dma((chunks, planes, side)), dma((chunks, n)),
        ],
        compiler_params=pltpu.CompilerParams(
            collective_id=0, has_side_effects=True, vmem_limit_bytes=56 * 2**20
        ),
    )(pair, flat, flat, tri_in, tri_gate, tri_out, att_in, att_bias.T)

    def whole(shape):
        return pl.BlockSpec(shape, lambda i: (0,) * len(shape))

    def row(*shape):
        return pl.BlockSpec((1,) + shape, lambda i: (i, 0, 0))

    return pl.pallas_call(
        functools.partial(attention_kernel, rows, heads),
        grid=(rows,),
        out_shape=jax.ShapeDtypeStruct((rows, residues, width), f32),
        in_specs=[
            whole((chunks, n, heads * chunk, residues)), whole((1, residues)), smem,
            row(width, residues), row(3 * hd, residues), row(hd, residues), whole((hd, width)),
        ],
        out_specs=row(residues, width),
        scratch_shapes=[
            pltpu.VMEM((tiles, n * heads * chunk, 128), f32),
            pltpu.VMEM((heads, tiles, residues, 128), f32),
            pltpu.VMEM((heads, residues, residues), f32),
            pltpu.VMEM((width, hd), bf),
        ],
        compiler_params=pltpu.CompilerParams(vmem_limit_bytes=48 * 2**20),
    )(bias, flat, flat, pair1, qkv, gates, att_out)


def layer_norm(value):
    center = value - jnp.mean(value, axis=-1, keepdims=True)
    return center / jnp.sqrt(jnp.mean(center * center, axis=-1, keepdims=True) + 1e-05)


def per_device(pair, mask, tri_in, tri_gate, tri_out, att_in, att_bias, att_out):
    own_rows = pair.shape[0]
    residues = pair.shape[1]
    width = pair.shape[2]
    heads = att_bias.shape[1]
    head_size = att_out.shape[0] // heads
    valid = mask.astype(jnp.float32)
    start_row = lax.axis_index("row") * own_rows
    row_valid = lax.dynamic_slice_in_dim(valid, start_row, own_rows, 0)
    pair_mask = row_valid[:, None] * valid[None, :]
    normed = layer_norm(pair).astype(jnp.bfloat16)
    proj = jnp.einsum("rkc,cf->rkf", normed, tri_in, preferred_element_type=jnp.float32)
    left = (
        jax.nn.sigmoid(proj[..., width : 2 * width]) * proj[..., :width] * pair_mask[..., None]
    ).astype(jnp.bfloat16)
    right = (
        jax.nn.sigmoid(proj[..., 3 * width :])
        * proj[..., 2 * width : 3 * width]
        * pair_mask[..., None]
    ).astype(jnp.bfloat16)
    left_by_channel = jnp.transpose(left, (2, 0, 1))
    right_by_channel = jnp.transpose(right, (2, 0, 1))
    left_all, right_all = (
        lax.all_to_all(left_by_channel, "row", split_axis=0, concat_axis=1, tiled=True),
        lax.all_to_all(right_by_channel, "row", split_axis=0, concat_axis=1, tiled=True),
    )
    tri_channel = jnp.einsum(
        "cik,cjk->cij", left_all, right_all, preferred_element_type=jnp.float32
    )
    tri_rows = lax.all_to_all(
        tri_channel.astype(jnp.bfloat16), "row", split_axis=1, concat_axis=0, tiled=True
    ).astype(tri_channel.dtype)
    tri = jnp.transpose(tri_rows, (1, 2, 0))
    tnorm = layer_norm(tri).astype(jnp.bfloat16)
    update = jnp.einsum("rkc,cf->rkf", tnorm, tri_out, preferred_element_type=jnp.float32)
    gating = jax.nn.sigmoid(
        jnp.einsum("rkc,cf->rkf", normed, tri_gate, preferred_element_type=jnp.float32)
    )
    pair1 = pair + pair_mask[..., None] * gating * update
    ynorm = layer_norm(pair1).astype(jnp.bfloat16)
    qkvg = jnp.einsum("rkc,cf->rkf", ynorm, att_in, preferred_element_type=jnp.float32)
    qkvg = qkvg.reshape(own_rows, residues, 4, heads, head_size)
    query = qkvg[:, :, 0].astype(jnp.bfloat16)
    keys = qkvg[:, :, 1].astype(jnp.bfloat16)
    values = qkvg[:, :, 2].astype(jnp.bfloat16)
    gates = qkvg[:, :, 3]
    local_bias = jnp.einsum(
        "rkc,ch->hrk", ynorm, att_bias, preferred_element_type=jnp.float32
    ).astype(jnp.bfloat16)
    bias = lax.all_gather(local_bias, "row", axis=1, tiled=True)
    scores = jnp.einsum(
        "ijhd,ikhd->ihjk", query, keys, preferred_element_type=jnp.float32
    ) / jnp.sqrt(jnp.float32(head_size))
    scores = scores + bias.astype(jnp.float32)[None]
    scores = jnp.where(mask[None, None, None, :] > 0, scores, jnp.float32(-1000000000.0))
    probs = jax.nn.softmax(scores, axis=-1).astype(jnp.bfloat16)
    mixed = jnp.einsum("ihjk,ikhd->ijhd", probs, values, preferred_element_type=jnp.float32)
    att = (
        (jax.nn.sigmoid(gates) * mixed)
        .astype(jnp.bfloat16)
        .reshape(own_rows, residues, heads * head_size)
    )
    out = jnp.einsum("rkf,fc->rkc", att, att_out, preferred_element_type=jnp.float32)
    return pair1 + row_valid[:, None, None] * out


def solution(mesh):
    n = mesh.shape["row"]

    def per_shard(pair, mask, tri_in, tri_gate, tri_out, att_in, att_bias, att_out):
        rows, residues, width = pair.shape
        fits = (
            width % n == 0 and n % PLANE == 0 and n % 16 == 0 and residues % 128 == 0
            and chunk_rows(n, rows, width, att_bias.shape[1]) > 0
        )
        run = functools.partial(fused, n) if fits else per_device
        return run(pair, mask, tri_in, tri_gate, tri_out, att_in, att_bias, att_out)

    return jax.shard_map(
        per_shard,
        mesh=mesh,
        in_specs=(P(("groups", "row"), None, None), P("groups"), P(), P(), P(), P(), P(), P()),
        out_specs=P(("groups", "row"), None, None),
        check_vma=False,
    )
```

```python
import functools
import math

import jax
import jax.numpy as jnp
from jax import lax
from jax.experimental import pallas as pl
from jax.experimental.pallas import tpu as pltpu
from jax.sharding import PartitionSpec as P

EPS = 1e-05
LOG2E = math.log2(math.e)
MESH = pl.DeviceIdType.MESH
PLANE = 8


def sigmoid(value):
    return 0.5 * jnp.tanh(0.5 * value) + 0.5


def norm_rows(value):
    center = value - jnp.mean(value, axis=0, keepdims=True)
    return center * lax.rsqrt(jnp.mean(center * center, axis=0, keepdims=True) + EPS)


def scatter_rows(ref, first, stride, value):
    for q in range(ref.shape[0]):
        ref[q, pl.ds(first, value.shape[0], stride=stride), :] = value[:, q * 128 : (q + 1) * 128]


def gather_rows(ref, first, count, stride):
    parts = [ref[q, pl.ds(first, count, stride=stride), :] for q in range(ref.shape[0])]
    return jnp.concatenate(parts, axis=1)


def all_rows(ref):
    return jnp.concatenate([ref[q] for q in range(ref.shape[0])], axis=1)


def matmul(a, b):
    return jnp.dot(a, b, preferred_element_type=jnp.float32)


def to_t(ref):
    return ref[...].astype(jnp.float32).T.astype(jnp.bfloat16)


def triangle_kernel(
    n, chunk, heads,
    pair_ref, mask_ref, live_ref, tri_in_ref, gate_ref, tri_out_ref, att_in_ref, bias_w_ref,
    pair1_ref, qkv_ref, g_ref, bias_ref,
    wide, bias_wide, bias_rows, right_mat, xn, yn, gating, tri_in_t, gate_t, tri_out_t, att_in_t,
    left_send, right_send, tri_send, left_got, right_got, tri_got, bias_all,
    left_ssem, left_rsem, right_ssem, right_rsem, tri_ssem, tri_rsem,
    z_ssem, plane_ssem, core_ssem, bias_rsem,
):
    rows, residues, width = pair_ref.shape
    per = width // n
    block = per * chunk
    chunks = rows // chunk
    hd = g_ref.shape[1]
    tiles = residues // 128
    me = lax.axis_index("row")
    group = lax.axis_index("groups")

    def loop(low, high, body):
        def step(i, _):
            body(i)
            return 0
        lax.fori_loop(low, high, step, 0)

    def peer(t):
        return lax.rem(me + (t % 2) * (n // 2) + t // 2, n)

    def copy_to(src, dst, ssem, rsem, device):
        return pltpu.make_async_remote_copy(
            src_ref=src, dst_ref=dst, send_sem=ssem, recv_sem=rsem,
            device_id=(group, device), device_id_type=MESH,
        )

    def outgoing(plan, u, d):
        send, got, ssem, rsem = plan
        return copy_to(send.at[u, d], got.at[u, me], ssem.at[u, d], rsem.at[u, me], d)

    def incoming(plan, u, s):
        send, got, ssem, rsem = plan
        return copy_to(send.at[u, s], got.at[u, s], ssem.at[u, s], rsem.at[u, s], s)

    left = (left_send, left_got, left_ssem, left_rsem)
    right = (right_send, right_got, right_ssem, right_rsem)
    back = (tri_send, tri_got, tri_ssem, tri_rsem)

    def send_chunk(plan, u):
        def narrow(d):
            for q in range(tiles):
                part = wide[q, pl.ds(pl.multiple_of(d * block, 16), block), :]
                plan[0][u, d, :, q * 128 : (q + 1) * 128] = part.astype(jnp.bfloat16)
        loop(0, n, narrow)
        loop(1, n, lambda t: outgoing(plan, u, peer(t)).start())
        plan[1][u, me] = plan[0][u, me]

    def receive_chunk(plan, u):
        loop(1, n, lambda t: incoming(plan, u, lax.rem(me + t, n)).wait_recv())

        def widen(s):
            for q in range(tiles):
                part = plan[1][u, s, :, q * 128 : (q + 1) * 128].astype(jnp.float32)
                wide[q, pl.ds(pl.multiple_of(s * block, 16), block), :] = part
        loop(0, n, widen)

    barrier = pltpu.get_barrier_semaphore()
    loop(1, n, lambda t: pl.semaphore_signal(
        barrier, inc=1, device_id=(group, lax.rem(me + t, n)), device_id_type=MESH))

    valid = mask_ref[...].astype(jnp.float32)

    def pm(r):
        return valid * live_ref[0, me * rows + r].astype(jnp.float32)

    tri_in_t[...] = to_t(tri_in_ref)

    def gated(r, place, first):
        proj = matmul(tri_in_t[first : first + 2 * width, :], xn[r])
        value = sigmoid(proj[width:]) * proj[:width] * pm(r)
        scatter_rows(wide, place, chunk, value)

    for u in range(chunks):
        def right_row(t):
            r = u * chunk + t
            pair_t = jnp.concatenate(
                [pair_ref[r, pl.ds(rr, n, stride=rows), :] for rr in range(rows)], axis=0
            ).T
            pair1_ref[r] = pair_t
            xn[r] = norm_rows(pair_t).astype(jnp.bfloat16)
            gated(r, t, 2 * width)
        loop(0, chunk, right_row)
        if u == 0:
            pl.semaphore_wait(barrier, n - 1)
        send_chunk(right, u)
    for u in range(chunks):
        loop(0, chunk, lambda t: gated(u * chunk + t, t, 0))
        send_chunk(left, u)

    gate_t[...] = to_t(gate_ref)
    tri_out_t[...] = to_t(tri_out_ref)
    att_in_t[...] = to_t(att_in_ref)

    def gate_row(r):
        gating[r] = sigmoid(matmul(gate_t[...], xn[r])) * pm(r)
    loop(0, rows, gate_row)

    for u in range(chunks):
        receive_chunk(right, u)
        for c in range(per):
            for t in range(chunk):
                first = (u * chunk + t) * n
                part = gather_rows(wide, c * chunk + t, n, block)
                right_mat[c, first : first + n, :] = part.astype(jnp.bfloat16)
    for u in range(chunks):
        receive_chunk(left, u)
        for c in range(per):
            lefts = [gather_rows(wide, c * chunk + t, n, block) for t in range(chunk)]
            tri = lax.dot_general(
                jnp.concatenate(lefts, axis=0).astype(jnp.bfloat16), right_mat[c],
                (((1,), (1,)), ((), ())), preferred_element_type=jnp.float32,
            )
            for t in range(chunk):
                scatter_rows(wide, c * chunk + t, block, tri[t * n : (t + 1) * n])
        send_chunk(back, u)

    planes = n // PLANE
    low = lax.rem(me, PLANE)
    base = me - low
    twin_low = low - lax.rem(me, 2) + (1 - lax.rem(me, 2))
    twin = base + twin_low

    def put(u, b, ssem, device):
        return copy_to(bias_all.at[u, b], bias_all.at[u, b], ssem, bias_rsem.at[u, b], device)

    def along(step):
        return lax.rem(me + step * PLANE, n)

    def beside(step):
        return base + lax.rem(low + 2 * step, PLANE)

    def bias_first(u):
        for step in range(1, planes):
            put(u, me, z_ssem.at[u, step], along(step)).start()

    def bias_second(u):
        for z in range(planes):
            b = along(z)
            if z:
                put(u, b, z_ssem.at[u, z], me).wait_recv()
            for step in range(1, PLANE // 2):
                put(u, b, plane_ssem.at[u, z, step], beside(step)).start()
            put(u, b, core_ssem.at[u, z, 0], twin).start()

    def bias_third(u):
        for z in range(planes):
            for step in range(1, PLANE // 2):
                b = lax.rem(beside(step) + z * PLANE, n)
                put(u, b, plane_ssem.at[u, z, step], me).wait_recv()
                put(u, b, core_ssem.at[u, z, step], twin).start()

    def bias_last(u):
        for z in range(planes):
            for step in range(PLANE // 2):
                b = lax.rem(base + lax.rem(twin_low + 2 * step, PLANE) + z * PLANE, n)
                put(u, b, core_ssem.at[u, z, step], me).wait_recv()

    hide = jnp.where(mask_ref[...] > 0, 0.0, -jnp.inf)

    def bias_finish(u):
        bias_last(u)
        tall = heads * chunk

        def widen(s):
            for q in range(tiles):
                part = bias_all[u, s, :, q * 128 : (q + 1) * 128].astype(jnp.float32)
                bias_rows[q, pl.ds(pl.multiple_of(s * tall, 16), tall), :] = part * LOG2E
        loop(0, n, widen)
        for h in range(heads):
            part = jnp.concatenate([gather_rows(bias_rows, h * chunk + t, n, tall) for t in range(chunk)], axis=0)
            bias_ref[h, :, u * chunk * n : (u + 1) * chunk * n] = (part + hide).T

    def bias_sent(u):
        for step in range(1, planes):
            put(u, me, z_ssem.at[u, step], along(step)).wait_send()
        for z in range(planes):
            for step in range(PLANE // 2):
                b = lax.rem(beside(step) + z * PLANE, n)
                put(u, b, core_ssem.at[u, z, step], twin).wait_send()
                if step:
                    put(u, along(z), plane_ssem.at[u, z, step], beside(step)).wait_send()

    scale = LOG2E / math.sqrt(hd // heads)

    def qkvg_row(r):
        qkvg = matmul(att_in_t[...], yn[r])
        qkv_ref[r, :hd, :] = (qkvg[:hd] * scale).astype(jnp.bfloat16)
        qkv_ref[r, hd:, :] = qkvg[hd : 3 * hd].astype(jnp.bfloat16)
        g_ref[r] = sigmoid(qkvg[3 * hd :])

    for u in range(chunks):
        receive_chunk(back, u)

        def pair_row(t):
            r = u * chunk + t
            tnorm = norm_rows(gather_rows(wide, t, width, chunk)).astype(jnp.bfloat16)
            pair1 = pair1_ref[r] + gating[r] * matmul(tri_out_t[...], tnorm)
            pair1_ref[r] = pair1
            fresh = norm_rows(pair1).astype(jnp.bfloat16)
            yn[r] = fresh
            scatter_rows(bias_wide, t, chunk, matmul(bias_w_ref[...], fresh))
        loop(0, chunk, pair_row)
        bias_all[u, me] = all_rows(bias_wide).astype(jnp.bfloat16)
        bias_first(u)
        if u < chunks - 1:
            loop(u * chunk, (u + 1) * chunk, qkvg_row)
        if u >= 1:
            bias_second(u - 1)
        if u >= 2:
            bias_third(u - 2)
    done = (chunks - 1) * chunk
    half = chunk // 2
    for u in range(chunks - 2):
        bias_finish(u)
    bias_second(chunks - 1)
    loop(done, done + half, qkvg_row)
    if chunks >= 2:
        bias_third(chunks - 2)
    bias_third(chunks - 1)
    loop(done + half, done + chunk, qkvg_row)
    for u in range(max(chunks - 2, 0), chunks):
        bias_finish(u)
    for u in range(chunks):
        bias_sent(u)
        for plan in (right, left, back):
            loop(1, n, lambda t: outgoing(plan, u, lax.rem(me + t, n)).wait_send())


def attention_kernel(n, bias_ref, live_ref, pair1_ref, qkv_ref, g_ref, att_out_ref, out_ref, out_t):
    heads, residues, _ = bias_ref.shape
    rows = residues // n
    hd = g_ref.shape[1]
    size = hd // heads

    @pl.when(pl.program_id(0) == 0)
    def _():
        out_t[...] = to_t(att_out_ref)

    ones = jnp.ones((16, residues), jnp.bfloat16)
    parts = []
    for h in range(heads):
        first = h * size
        query = qkv_ref[0, first : first + size, :]
        keys = qkv_ref[0, hd + first : hd + first + size, :]
        values = qkv_ref[0, 2 * hd + first : 2 * hd + first + size, :]
        scores = lax.dot_general(keys, query, (((0,), (0,)), ((), ())), preferred_element_type=jnp.float32)
        scores = scores + bias_ref[h]
        probs = jnp.exp2(scores - jnp.max(scores, axis=0, keepdims=True)).astype(jnp.bfloat16)
        mixed = matmul(jnp.concatenate([values, ones], axis=0), probs)
        gates = g_ref[0, first : first + size, :]
        parts.append((mixed[:size] * (1.0 / mixed[size : size + 1]) * gates).astype(jnp.bfloat16))
    out = matmul(out_t[...], jnp.concatenate(parts, axis=0))
    live = live_ref[0, lax.axis_index("row") * rows + pl.program_id(0)].astype(jnp.float32)
    new = (pair1_ref[0] + live * out).T
    for r in range(rows):
        out_ref[0, pl.ds(r, n, stride=rows), :] = new[r * n : (r + 1) * n]


def chunk_rows(n, rows, width, heads):
    per = width // n
    for chunk in range(1, rows + 1):
        if rows % chunk == 0 and (chunk * n) % 128 == 0 and (per * chunk) % 16 == 0 and (heads * chunk) % 16 == 0:
            return chunk
    return 0


def fused(n, pair, mask, tri_in, tri_gate, tri_out, att_in, att_bias, att_out):
    rows, residues, width = pair.shape
    heads = att_bias.shape[1]
    hd = att_out.shape[0]
    per = width // n
    chunk = chunk_rows(n, rows, width, heads)
    chunks = rows // chunk
    tiles = residues // 128
    planes = n // PLANE
    flat = mask.reshape(1, residues)
    turned = mask.reshape(n, rows).T.reshape(1, residues)
    bf, f32 = jnp.bfloat16, jnp.float32
    vmem = pl.BlockSpec(memory_space=pltpu.VMEM)
    smem = pl.BlockSpec(memory_space=pltpu.SMEM)
    dma = pltpu.SemaphoreType.DMA
    blocks = pltpu.VMEM((chunks, n, per * chunk, residues), bf)
    side = PLANE // 2
    pair1, qkv, gates, bias = pl.pallas_call(
        functools.partial(triangle_kernel, n, chunk, heads),
        out_shape=(
            jax.ShapeDtypeStruct((rows, width, residues), f32),
            jax.ShapeDtypeStruct((rows, 3 * hd, residues), bf),
            jax.ShapeDtypeStruct((rows, hd, residues), f32),
            jax.ShapeDtypeStruct((heads, residues, residues), f32),
        ),
        in_specs=[vmem, vmem, smem] + [vmem] * 5,
        out_specs=(vmem,) * 4,
        scratch_shapes=[
            pltpu.VMEM((tiles, width * chunk, 128), f32),
            pltpu.VMEM((tiles, heads * chunk, 128), f32),
            pltpu.VMEM((tiles, n * heads * chunk, 128), f32),
            pltpu.VMEM((per, residues, residues), bf),
            pltpu.VMEM((rows, width, residues), bf),
            pltpu.VMEM((rows, width, residues), bf),
            pltpu.VMEM((rows, width, residues), f32),
            pltpu.VMEM((4 * width, width), bf),
            pltpu.VMEM((width, width), bf),
            pltpu.VMEM((width, width), bf),
            pltpu.VMEM((4 * hd, width), bf),
        ] + [blocks] * 6 + [
            pltpu.VMEM((chunks, n, heads * chunk, residues), bf),
        ] + [dma((chunks, n))] * 6 + [
            dma((chunks, planes)), dma((chunks, planes, side)), dma((chunks, planes, side)), dma((chunks, n)),
        ],
        compiler_params=pltpu.CompilerParams(
            collective_id=0, has_side_effects=True, vmem_limit_bytes=60 * 2**20
        ),
    )(pair, turned, flat, tri_in, tri_gate, tri_out, att_in, att_bias.T)

    def whole(shape):
        return pl.BlockSpec(shape, lambda i: (0,) * len(shape))

    def row(*shape):
        return pl.BlockSpec((1,) + shape, lambda i: (i, 0, 0))

    return pl.pallas_call(
        functools.partial(attention_kernel, n),
        grid=(rows,),
        out_shape=jax.ShapeDtypeStruct((rows, residues, width), f32),
        in_specs=[
            whole((heads, residues, residues)), smem,
            row(width, residues), row(3 * hd, residues), row(hd, residues), whole((hd, width)),
        ],
        out_specs=row(residues, width),
        scratch_shapes=[
            pltpu.VMEM((width, hd), bf),
        ],
        compiler_params=pltpu.CompilerParams(vmem_limit_bytes=60 * 2**20),
    )(bias, flat, pair1, qkv, gates, att_out)


def layer_norm(value):
    center = value - jnp.mean(value, axis=-1, keepdims=True)
    return center / jnp.sqrt(jnp.mean(center * center, axis=-1, keepdims=True) + 1e-05)


def per_device(pair, mask, tri_in, tri_gate, tri_out, att_in, att_bias, att_out):
    own_rows = pair.shape[0]
    residues = pair.shape[1]
    width = pair.shape[2]
    heads = att_bias.shape[1]
    head_size = att_out.shape[0] // heads
    valid = mask.astype(jnp.float32)
    start_row = lax.axis_index("row") * own_rows
    row_valid = lax.dynamic_slice_in_dim(valid, start_row, own_rows, 0)
    pair_mask = row_valid[:, None] * valid[None, :]
    normed = layer_norm(pair).astype(jnp.bfloat16)
    proj = jnp.einsum("rkc,cf->rkf", normed, tri_in, preferred_element_type=jnp.float32)
    left = (
        jax.nn.sigmoid(proj[..., width : 2 * width]) * proj[..., :width] * pair_mask[..., None]
    ).astype(jnp.bfloat16)
    right = (
        jax.nn.sigmoid(proj[..., 3 * width :])
        * proj[..., 2 * width : 3 * width]
        * pair_mask[..., None]
    ).astype(jnp.bfloat16)
    left_by_channel = jnp.transpose(left, (2, 0, 1))
    right_by_channel = jnp.transpose(right, (2, 0, 1))
    left_all, right_all = (
        lax.all_to_all(left_by_channel, "row", split_axis=0, concat_axis=1, tiled=True),
        lax.all_to_all(right_by_channel, "row", split_axis=0, concat_axis=1, tiled=True),
    )
    tri_channel = jnp.einsum(
        "cik,cjk->cij", left_all, right_all, preferred_element_type=jnp.float32
    )
    tri_rows = lax.all_to_all(
        tri_channel.astype(jnp.bfloat16), "row", split_axis=1, concat_axis=0, tiled=True
    ).astype(tri_channel.dtype)
    tri = jnp.transpose(tri_rows, (1, 2, 0))
    tnorm = layer_norm(tri).astype(jnp.bfloat16)
    update = jnp.einsum("rkc,cf->rkf", tnorm, tri_out, preferred_element_type=jnp.float32)
    gating = jax.nn.sigmoid(
        jnp.einsum("rkc,cf->rkf", normed, tri_gate, preferred_element_type=jnp.float32)
    )
    pair1 = pair + pair_mask[..., None] * gating * update
    ynorm = layer_norm(pair1).astype(jnp.bfloat16)
    qkvg = jnp.einsum("rkc,cf->rkf", ynorm, att_in, preferred_element_type=jnp.float32)
    qkvg = qkvg.reshape(own_rows, residues, 4, heads, head_size)
    query = qkvg[:, :, 0].astype(jnp.bfloat16)
    keys = qkvg[:, :, 1].astype(jnp.bfloat16)
    values = qkvg[:, :, 2].astype(jnp.bfloat16)
    gates = qkvg[:, :, 3]
    local_bias = jnp.einsum(
        "rkc,ch->hrk", ynorm, att_bias, preferred_element_type=jnp.float32
    ).astype(jnp.bfloat16)
    bias = lax.all_gather(local_bias, "row", axis=1, tiled=True)
    scores = jnp.einsum(
        "ijhd,ikhd->ihjk", query, keys, preferred_element_type=jnp.float32
    ) / jnp.sqrt(jnp.float32(head_size))
    scores = scores + bias.astype(jnp.float32)[None]
    scores = jnp.where(mask[None, None, None, :] > 0, scores, jnp.float32(-1000000000.0))
    probs = jax.nn.softmax(scores, axis=-1).astype(jnp.bfloat16)
    mixed = jnp.einsum("ihjk,ikhd->ijhd", probs, values, preferred_element_type=jnp.float32)
    att = (
        (jax.nn.sigmoid(gates) * mixed)
        .astype(jnp.bfloat16)
        .reshape(own_rows, residues, heads * head_size)
    )
    out = jnp.einsum("rkf,fc->rkc", att, att_out, preferred_element_type=jnp.float32)
    return pair1 + row_valid[:, None, None] * out


def solution(mesh):
    n = mesh.shape["row"]

    def per_shard(pair, mask, tri_in, tri_gate, tri_out, att_in, att_bias, att_out):
        rows, residues, width = pair.shape
        fits = (
            rows * n == residues and width % n == 0 and n % PLANE == 0 and n % 16 == 0 and residues % 128 == 0
            and chunk_rows(n, rows, width, att_bias.shape[1]) > 0
        )
        run = functools.partial(fused, n) if fits else per_device
        return run(pair, mask, tri_in, tri_gate, tri_out, att_in, att_bias, att_out)

    return jax.shard_map(
        per_shard,
        mesh=mesh,
        in_specs=(P(("groups", "row"), None, None), P("groups"), P(), P(), P(), P(), P(), P()),
        out_specs=P(("groups", "row"), None, None),
        check_vma=False,
    )
```

```python
import functools
import math

import jax
import jax.numpy as jnp
from jax import lax
from jax.experimental import pallas as pl
from jax.experimental.pallas import tpu as pltpu
from jax.sharding import PartitionSpec as P

EPS = 1e-05
LOG2E = math.log2(math.e)
MESH = pl.DeviceIdType.MESH
PLANE = 8


def sigmoid(value):
    return 0.5 * jnp.tanh(0.5 * value) + 0.5


def norm_rows(value):
    center = value - jnp.mean(value, axis=0, keepdims=True)
    return center * lax.rsqrt(jnp.mean(center * center, axis=0, keepdims=True) + EPS)


def scatter_rows(ref, first, stride, value):
    for q in range(ref.shape[0]):
        ref[q, pl.ds(first, value.shape[0], stride=stride), :] = value[:, q * 128 : (q + 1) * 128]


def gather_rows(ref, first, count, stride):
    parts = [ref[q, pl.ds(first, count, stride=stride), :] for q in range(ref.shape[0])]
    return jnp.concatenate(parts, axis=1)


def all_rows(ref):
    return jnp.concatenate([ref[q] for q in range(ref.shape[0])], axis=1)


def matmul(a, b):
    return jnp.dot(a, b, preferred_element_type=jnp.float32)


def to_t(ref):
    return ref[...].astype(jnp.float32).T.astype(jnp.bfloat16)


def triangle_kernel(
    n, chunk, heads,
    pair_hbm, mask_ref, tri_in_ref, gate_ref, tri_out_ref, att_in_ref, bias_w_ref,
    pair1_hbm, qkv_hbm, g_hbm, bias_ref,
    pair_ref, pair1_ref, qkv_ref, g_ref, pair_sem, out_sem,
    wide, bias_wide, bias_rows, right_mat, xn, yn, gating, tri_in_t, gate_t, tri_out_t, att_in_t,
    left_send, right_send, tri_send, left_got, right_got, tri_got, bias_all,
    left_ssem, left_rsem, right_ssem, right_rsem, tri_ssem, tri_rsem,
    z_ssem, plane_ssem, core_ssem, bias_rsem,
):
    rows, residues, width = pair_ref.shape
    for u in range(rows // chunk):
        at = pl.ds(u * chunk, chunk)
        pltpu.make_async_copy(pair_hbm.at[at], pair_ref.at[at], pair_sem.at[u]).start()
    per = width // n
    block = per * chunk
    chunks = rows // chunk
    hd = g_ref.shape[1]
    tiles = residues // 128
    me = lax.axis_index("row")
    group = lax.axis_index("groups")

    def loop(low, high, body):
        def step(i, _):
            body(i)
            return 0
        lax.fori_loop(low, high, step, 0)

    def peer(t):
        return lax.rem(me + (t % 2) * (n // 2) + t // 2, n)

    def copy_to(src, dst, ssem, rsem, device):
        return pltpu.make_async_remote_copy(
            src_ref=src, dst_ref=dst, send_sem=ssem, recv_sem=rsem,
            device_id=(group, device), device_id_type=MESH,
        )

    def outgoing(plan, u, d):
        send, got, ssem, rsem = plan
        return copy_to(send.at[u, d], got.at[u, me], ssem.at[u, d], rsem.at[u, me], d)

    def incoming(plan, u, s):
        send, got, ssem, rsem = plan
        return copy_to(send.at[u, s], got.at[u, s], ssem.at[u, s], rsem.at[u, s], s)

    left = (left_send, left_got, left_ssem, left_rsem)
    right = (right_send, right_got, right_ssem, right_rsem)
    back = (tri_send, tri_got, tri_ssem, tri_rsem)

    def send_chunk(plan, u):
        def narrow(d):
            for q in range(tiles):
                part = wide[q, pl.ds(pl.multiple_of(d * block, 16), block), :]
                plan[0][u, d, :, q * 128 : (q + 1) * 128] = part.astype(jnp.bfloat16)
        loop(0, n, narrow)
        loop(1, n, lambda t: outgoing(plan, u, peer(t)).start())
        plan[1][u, me] = plan[0][u, me]

    def receive_chunk(plan, u):
        loop(1, n, lambda t: incoming(plan, u, lax.rem(me + t, n)).wait_recv())

        def widen(s):
            for q in range(tiles):
                part = plan[1][u, s, :, q * 128 : (q + 1) * 128].astype(jnp.float32)
                wide[q, pl.ds(pl.multiple_of(s * block, 16), block), :] = part
        loop(0, n, widen)

    barrier = pltpu.get_barrier_semaphore()
    loop(1, n, lambda t: pl.semaphore_signal(
        barrier, inc=1, device_id=(group, lax.rem(me + t, n)), device_id_type=MESH))

    length = lax.fori_loop(0, residues, lambda i, total: total + mask_ref[i], jnp.int32(0))
    place = lax.broadcasted_iota(jnp.int32, (1, residues), 1)
    natural = lax.rem(place, n) * rows + place // n
    valid = jnp.where(natural < length, 1.0, 0.0)

    def pm(r):
        return valid * mask_ref[me * rows + r].astype(jnp.float32)

    tri_in_t[...] = to_t(tri_in_ref)

    def gated(r, place, first):
        proj = matmul(tri_in_t[first : first + 2 * width, :], xn[r])
        value = sigmoid(proj[width:]) * proj[:width] * pm(r)
        scatter_rows(wide, place, chunk, value)

    for u in range(chunks):
        at = pl.ds(u * chunk, chunk)
        pltpu.make_async_copy(pair_hbm.at[at], pair_ref.at[at], pair_sem.at[u]).wait()

        def right_row(t):
            r = u * chunk + t
            pair_t = jnp.concatenate(
                [pair_ref[r, pl.ds(rr, n, stride=rows), :] for rr in range(rows)], axis=0
            ).T
            pair1_ref[r] = pair_t
            xn[r] = norm_rows(pair_t).astype(jnp.bfloat16)
            gated(r, t, 2 * width)
        loop(0, chunk, right_row)
        if u == 0:
            pl.semaphore_wait(barrier, n - 1)
        send_chunk(right, u)
    for u in range(chunks):
        loop(0, chunk, lambda t: gated(u * chunk + t, t, 0))
        send_chunk(left, u)

    gate_t[...] = to_t(gate_ref)
    tri_out_t[...] = to_t(tri_out_ref)
    att_in_t[...] = to_t(att_in_ref)

    def gate_row(r):
        gating[r] = sigmoid(matmul(gate_t[...], xn[r])) * pm(r)
    loop(0, rows, gate_row)

    for u in range(chunks):
        receive_chunk(right, u)
        for c in range(per):
            for t in range(chunk):
                first = (u * chunk + t) * n
                part = gather_rows(wide, c * chunk + t, n, block)
                right_mat[c, first : first + n, :] = part.astype(jnp.bfloat16)
    for u in range(chunks):
        receive_chunk(left, u)
        for c in range(per):
            lefts = [gather_rows(wide, c * chunk + t, n, block) for t in range(chunk)]
            tri = lax.dot_general(
                jnp.concatenate(lefts, axis=0).astype(jnp.bfloat16), right_mat[c],
                (((1,), (1,)), ((), ())), preferred_element_type=jnp.float32,
            )
            for t in range(chunk):
                scatter_rows(wide, c * chunk + t, block, tri[t * n : (t + 1) * n])
        send_chunk(back, u)

    planes = n // PLANE
    low = lax.rem(me, PLANE)
    base = me - low
    twin_low = low - lax.rem(me, 2) + (1 - lax.rem(me, 2))
    twin = base + twin_low

    def put(u, b, ssem, device):
        return copy_to(bias_all.at[u, b], bias_all.at[u, b], ssem, bias_rsem.at[u, b], device)

    def along(step):
        return lax.rem(me + step * PLANE, n)

    def beside(step):
        return base + lax.rem(low + 2 * step, PLANE)

    def bias_first(u):
        for step in range(1, planes):
            put(u, me, z_ssem.at[u, step], along(step)).start()

    def bias_second(u):
        for z in range(planes):
            b = along(z)
            if z:
                put(u, b, z_ssem.at[u, z], me).wait_recv()
            for step in range(1, PLANE // 2):
                put(u, b, plane_ssem.at[u, z, step], beside(step)).start()
            put(u, b, core_ssem.at[u, z, 0], twin).start()

    def bias_third(u):
        for z in range(planes):
            for step in range(1, PLANE // 2):
                b = lax.rem(beside(step) + z * PLANE, n)
                put(u, b, plane_ssem.at[u, z, step], me).wait_recv()
                put(u, b, core_ssem.at[u, z, step], twin).start()

    def bias_last(u):
        for z in range(planes):
            for step in range(PLANE // 2):
                b = lax.rem(base + lax.rem(twin_low + 2 * step, PLANE) + z * PLANE, n)
                put(u, b, core_ssem.at[u, z, step], me).wait_recv()

    hide = jnp.where(natural < length, 0.0, -jnp.inf)

    def bias_finish(u):
        bias_last(u)
        tall = heads * chunk

        def widen(s):
            for q in range(tiles):
                part = bias_all[u, s, :, q * 128 : (q + 1) * 128].astype(jnp.float32)
                bias_rows[q, pl.ds(pl.multiple_of(s * tall, 16), tall), :] = part * LOG2E
        loop(0, n, widen)
        for h in range(heads):
            part = jnp.concatenate([gather_rows(bias_rows, h * chunk + t, n, tall) for t in range(chunk)], axis=0)
            bias_ref[h, :, u * chunk * n : (u + 1) * chunk * n] = (part + hide).T

    def bias_sent(u):
        for step in range(1, planes):
            put(u, me, z_ssem.at[u, step], along(step)).wait_send()
        for z in range(planes):
            for step in range(PLANE // 2):
                b = lax.rem(beside(step) + z * PLANE, n)
                put(u, b, core_ssem.at[u, z, step], twin).wait_send()
                if step:
                    put(u, along(z), plane_ssem.at[u, z, step], beside(step)).wait_send()

    scale = LOG2E / math.sqrt(hd // heads)

    def qkvg_row(r):
        qkvg = matmul(att_in_t[...], yn[r])
        qkv_ref[r, :hd, :] = (qkvg[:hd] * scale).astype(jnp.bfloat16)
        qkv_ref[r, hd:, :] = qkvg[hd : 3 * hd].astype(jnp.bfloat16)
        g_ref[r] = sigmoid(qkvg[3 * hd :])

    def store(u):
        at = pl.ds(u * chunk, chunk)
        pairs = ((pair1_ref, pair1_hbm), (qkv_ref, qkv_hbm), (g_ref, g_hbm))
        return [pltpu.make_async_copy(v.at[at], h.at[at], out_sem.at[u, k]) for k, (v, h) in enumerate(pairs)]

    for u in range(chunks):
        receive_chunk(back, u)

        def pair_row(t):
            r = u * chunk + t
            tnorm = norm_rows(gather_rows(wide, t, width, chunk)).astype(jnp.bfloat16)
            pair1 = pair1_ref[r] + gating[r] * matmul(tri_out_t[...], tnorm)
            pair1_ref[r] = pair1
            fresh = norm_rows(pair1).astype(jnp.bfloat16)
            yn[r] = fresh
            scatter_rows(bias_wide, t, chunk, matmul(bias_w_ref[...], fresh))
        loop(0, chunk, pair_row)
        bias_all[u, me] = all_rows(bias_wide).astype(jnp.bfloat16)
        bias_first(u)
        if u < chunks - 1:
            loop(u * chunk, (u + 1) * chunk, qkvg_row)
            for copy in store(u):
                copy.start()
        if u >= 1:
            bias_second(u - 1)
        if u >= 2:
            bias_third(u - 2)
    done = (chunks - 1) * chunk
    half = chunk // 2
    for u in range(chunks - 2):
        bias_finish(u)
    bias_second(chunks - 1)
    loop(done, done + half, qkvg_row)
    if chunks >= 2:
        bias_third(chunks - 2)
    bias_third(chunks - 1)
    loop(done + half, done + chunk, qkvg_row)
    for copy in store(chunks - 1):
        copy.start()
    for u in range(max(chunks - 2, 0), chunks):
        bias_finish(u)
    for u in range(chunks):
        bias_sent(u)
        for copy in store(u):
            copy.wait()
        for plan in (right, left, back):
            loop(1, n, lambda t: outgoing(plan, u, lax.rem(me + t, n)).wait_send())


def attention_kernel(n, bias_ref, live_ref, pair1_ref, qkv_ref, g_ref, att_out_ref, out_ref, out_t):
    heads, residues, _ = bias_ref.shape
    rows = residues // n
    hd = g_ref.shape[1]
    size = hd // heads

    @pl.when(pl.program_id(0) == 0)
    def _():
        out_t[...] = to_t(att_out_ref)

    ones = jnp.ones((16, residues), jnp.bfloat16)
    for i in range(out_ref.shape[0]):
        parts = []
        for h in range(heads):
            first = h * size
            query = qkv_ref[i, first : first + size, :]
            values = qkv_ref[i, 2 * hd + first : 2 * hd + first + size, :]
            keys = qkv_ref[i, hd + first : hd + first + size, :]
            scores = lax.dot_general(keys, query, (((0,), (0,)), ((), ())), preferred_element_type=jnp.float32)
            scores = scores + bias_ref[h]
            probs = jnp.exp2(scores - jnp.max(scores, axis=0, keepdims=True)).astype(jnp.bfloat16)
            mixed = matmul(jnp.concatenate([values, ones], axis=0), probs)
            gates = g_ref[i, first : first + size, :]
            parts.append((mixed[:size] * (1.0 / mixed[size : size + 1]) * gates).astype(jnp.bfloat16))
        out = matmul(out_t[...], jnp.concatenate(parts, axis=0))
        own = lax.axis_index("row") * rows + pl.program_id(0) * out_ref.shape[0] + i
        new = (pair1_ref[i] + live_ref[own].astype(jnp.float32) * out).T
        for r in range(rows):
            out_ref[i, pl.ds(r, n, stride=rows), :] = new[r * n : (r + 1) * n]


def chunk_rows(n, rows, width, heads):
    per = width // n
    for chunk in range(1, rows + 1):
        if rows % chunk == 0 and (chunk * n) % 128 == 0 and (per * chunk) % 16 == 0 and (heads * chunk) % 16 == 0:
            return chunk
    return 0


def fused(n, pair, mask, tri_in, tri_gate, tri_out, att_in, att_bias, att_out):
    rows, residues, width = pair.shape
    heads = att_bias.shape[1]
    hd = att_out.shape[0]
    per = width // n
    chunk = chunk_rows(n, rows, width, heads)
    chunks = rows // chunk
    tiles = residues // 128
    planes = n // PLANE
    bf, f32 = jnp.bfloat16, jnp.float32
    vmem = pl.BlockSpec(memory_space=pltpu.VMEM)
    smem = pl.BlockSpec(memory_space=pltpu.SMEM)
    hbm = pl.BlockSpec(memory_space=pl.ANY)
    dma = pltpu.SemaphoreType.DMA
    blocks = pltpu.VMEM((chunks, n, per * chunk, residues), bf)
    side = PLANE // 2
    many = 3 if rows % 3 == 0 else 1
    pair1, qkv, gates, bias = pl.pallas_call(
        functools.partial(triangle_kernel, n, chunk, heads),
        out_shape=(
            jax.ShapeDtypeStruct((rows, width, residues), f32),
            jax.ShapeDtypeStruct((rows, 3 * hd, residues), bf),
            jax.ShapeDtypeStruct((rows, hd, residues), f32),
            jax.ShapeDtypeStruct((heads, residues, residues), f32),
        ),
        in_specs=[hbm, smem] + [vmem] * 5,
        out_specs=(hbm, hbm, hbm, vmem),
        scratch_shapes=[
            pltpu.VMEM((rows, residues, width), f32),
            pltpu.VMEM((rows, width, residues), f32),
            pltpu.VMEM((rows, 3 * hd, residues), bf),
            pltpu.VMEM((rows, hd, residues), f32),
            dma((chunks,)),
            dma((chunks, 3)),
            pltpu.VMEM((tiles, width * chunk, 128), f32),
            pltpu.VMEM((tiles, heads * chunk, 128), f32),
            pltpu.VMEM((tiles, n * heads * chunk, 128), f32),
            pltpu.VMEM((per, residues, residues), bf),
            pltpu.VMEM((rows, width, residues), bf),
            pltpu.VMEM((rows, width, residues), bf),
            pltpu.VMEM((rows, width, residues), f32),
            pltpu.VMEM((4 * width, width), bf),
            pltpu.VMEM((width, width), bf),
            pltpu.VMEM((width, width), bf),
            pltpu.VMEM((4 * hd, width), bf),
        ] + [blocks] * 6 + [
            pltpu.VMEM((chunks, n, heads * chunk, residues), bf),
        ] + [dma((chunks, n))] * 6 + [
            dma((chunks, planes)), dma((chunks, planes, side)), dma((chunks, planes, side)), dma((chunks, n)),
        ],
        compiler_params=pltpu.CompilerParams(
            collective_id=0, has_side_effects=True, vmem_limit_bytes=60 * 2**20
        ),
    )(pair, mask, tri_in, tri_gate, tri_out, att_in, att_bias.T)

    def whole(shape):
        return pl.BlockSpec(shape, lambda i: (0,) * len(shape))

    def row(*shape):
        return pl.BlockSpec((many,) + shape, lambda i: (i, 0, 0))

    return pl.pallas_call(
        functools.partial(attention_kernel, n),
        grid=(rows // many,),
        out_shape=jax.ShapeDtypeStruct((rows, residues, width), f32),
        in_specs=[
            whole((heads, residues, residues)), smem,
            row(width, residues), row(3 * hd, residues), row(hd, residues), whole((hd, width)),
        ],
        out_specs=row(residues, width),
        scratch_shapes=[
            pltpu.VMEM((width, hd), bf),
        ],
        compiler_params=pltpu.CompilerParams(vmem_limit_bytes=60 * 2**20),
    )(bias, mask, pair1, qkv, gates, att_out)


def layer_norm(value):
    center = value - jnp.mean(value, axis=-1, keepdims=True)
    return center / jnp.sqrt(jnp.mean(center * center, axis=-1, keepdims=True) + 1e-05)


def per_device(pair, mask, tri_in, tri_gate, tri_out, att_in, att_bias, att_out):
    own_rows = pair.shape[0]
    residues = pair.shape[1]
    width = pair.shape[2]
    heads = att_bias.shape[1]
    head_size = att_out.shape[0] // heads
    valid = mask.astype(jnp.float32)
    start_row = lax.axis_index("row") * own_rows
    row_valid = lax.dynamic_slice_in_dim(valid, start_row, own_rows, 0)
    pair_mask = row_valid[:, None] * valid[None, :]
    normed = layer_norm(pair).astype(jnp.bfloat16)
    proj = jnp.einsum("rkc,cf->rkf", normed, tri_in, preferred_element_type=jnp.float32)
    left = (
        jax.nn.sigmoid(proj[..., width : 2 * width]) * proj[..., :width] * pair_mask[..., None]
    ).astype(jnp.bfloat16)
    right = (
        jax.nn.sigmoid(proj[..., 3 * width :])
        * proj[..., 2 * width : 3 * width]
        * pair_mask[..., None]
    ).astype(jnp.bfloat16)
    left_by_channel = jnp.transpose(left, (2, 0, 1))
    right_by_channel = jnp.transpose(right, (2, 0, 1))
    left_all, right_all = (
        lax.all_to_all(left_by_channel, "row", split_axis=0, concat_axis=1, tiled=True),
        lax.all_to_all(right_by_channel, "row", split_axis=0, concat_axis=1, tiled=True),
    )
    tri_channel = jnp.einsum(
        "cik,cjk->cij", left_all, right_all, preferred_element_type=jnp.float32
    )
    tri_rows = lax.all_to_all(
        tri_channel.astype(jnp.bfloat16), "row", split_axis=1, concat_axis=0, tiled=True
    ).astype(tri_channel.dtype)
    tri = jnp.transpose(tri_rows, (1, 2, 0))
    tnorm = layer_norm(tri).astype(jnp.bfloat16)
    update = jnp.einsum("rkc,cf->rkf", tnorm, tri_out, preferred_element_type=jnp.float32)
    gating = jax.nn.sigmoid(
        jnp.einsum("rkc,cf->rkf", normed, tri_gate, preferred_element_type=jnp.float32)
    )
    pair1 = pair + pair_mask[..., None] * gating * update
    ynorm = layer_norm(pair1).astype(jnp.bfloat16)
    qkvg = jnp.einsum("rkc,cf->rkf", ynorm, att_in, preferred_element_type=jnp.float32)
    qkvg = qkvg.reshape(own_rows, residues, 4, heads, head_size)
    query = qkvg[:, :, 0].astype(jnp.bfloat16)
    keys = qkvg[:, :, 1].astype(jnp.bfloat16)
    values = qkvg[:, :, 2].astype(jnp.bfloat16)
    gates = qkvg[:, :, 3]
    local_bias = jnp.einsum(
        "rkc,ch->hrk", ynorm, att_bias, preferred_element_type=jnp.float32
    ).astype(jnp.bfloat16)
    bias = lax.all_gather(local_bias, "row", axis=1, tiled=True)
    scores = jnp.einsum(
        "ijhd,ikhd->ihjk", query, keys, preferred_element_type=jnp.float32
    ) / jnp.sqrt(jnp.float32(head_size))
    scores = scores + bias.astype(jnp.float32)[None]
    scores = jnp.where(mask[None, None, None, :] > 0, scores, jnp.float32(-1000000000.0))
    probs = jax.nn.softmax(scores, axis=-1).astype(jnp.bfloat16)
    mixed = jnp.einsum("ihjk,ikhd->ijhd", probs, values, preferred_element_type=jnp.float32)
    att = (
        (jax.nn.sigmoid(gates) * mixed)
        .astype(jnp.bfloat16)
        .reshape(own_rows, residues, heads * head_size)
    )
    out = jnp.einsum("rkf,fc->rkc", att, att_out, preferred_element_type=jnp.float32)
    return pair1 + row_valid[:, None, None] * out


def solution(mesh):
    n = mesh.shape["row"]

    def per_shard(pair, mask, tri_in, tri_gate, tri_out, att_in, att_bias, att_out):
        rows, residues, width = pair.shape
        fits = (
            rows * n == residues and width % n == 0 and n % PLANE == 0 and n % 16 == 0 and residues % 128 == 0
            and chunk_rows(n, rows, width, att_bias.shape[1]) > 0
        )
        run = functools.partial(fused, n) if fits else per_device
        return run(pair, mask, tri_in, tri_gate, tri_out, att_in, att_bias, att_out)

    return jax.shard_map(
        per_shard,
        mesh=mesh,
        in_specs=(P(("groups", "row"), None, None), P("groups"), P(), P(), P(), P(), P(), P()),
        out_specs=P(("groups", "row"), None, None),
        check_vma=False,
    )
```

```python
import functools
import math

import jax
import jax.numpy as jnp
from jax import lax
from jax.experimental import pallas as pl
from jax.experimental.pallas import tpu as pltpu
from jax.sharding import PartitionSpec as P

EPS = 1e-05
LOG2E = math.log2(math.e)
MESH = pl.DeviceIdType.MESH
PLANE = 8


def sigmoid(value):
    return 0.5 * jnp.tanh(0.5 * value) + 0.5


def norm_rows(value):
    center = value - jnp.mean(value, axis=0, keepdims=True)
    return center * lax.rsqrt(jnp.mean(center * center, axis=0, keepdims=True) + EPS)


def scatter_rows(ref, first, stride, value):
    for q in range(ref.shape[0]):
        ref[q, pl.ds(first, value.shape[0], stride=stride), :] = value[:, q * 128 : (q + 1) * 128]


def gather_rows(ref, first, count, stride):
    parts = [ref[q, pl.ds(first, count, stride=stride), :] for q in range(ref.shape[0])]
    return jnp.concatenate(parts, axis=1)


def all_rows(ref):
    return jnp.concatenate([ref[q] for q in range(ref.shape[0])], axis=1)


def matmul(a, b):
    return jnp.dot(a, b, preferred_element_type=jnp.float32)


def to_t(ref):
    return ref[...].astype(jnp.float32).T.astype(jnp.bfloat16)


def triangle_kernel(
    n, chunk, heads,
    pair_hbm, mask_ref, tri_in_ref, gate_ref, tri_out_ref, att_in_ref, bias_w_ref,
    pair1_hbm, qkv_hbm, g_hbm, bias_ref,
    pair_ref, pair1_ref, qkv_ref, g_ref, pair_sem, out_sem,
    wide, bias_wide, bias_rows, right_mat, xn, yn, gating, tri_in_t, gate_t, tri_out_t, att_in_t,
    left_send, right_send, tri_send, left_got, right_got, tri_got, bias_all,
    left_ssem, left_rsem, right_ssem, right_rsem, tri_ssem, tri_rsem,
    z_ssem, plane_ssem, core_ssem, bias_rsem,
):
    rows, residues, width = pair_ref.shape
    for u in range(rows // chunk):
        at = pl.ds(u * chunk, chunk)
        pltpu.make_async_copy(pair_hbm.at[at], pair_ref.at[at], pair_sem.at[u]).start()
    per = width // n
    block = per * chunk
    chunks = rows // chunk
    hd = g_ref.shape[1]
    tiles = residues // 128
    me = lax.axis_index("row")
    group = lax.axis_index("groups")

    def loop(low, high, body):
        def step(i, _):
            body(i)
            return 0
        lax.fori_loop(low, high, step, 0)

    def peer(t):
        return lax.rem(me + (t % 2) * (n // 2) + t // 2, n)

    def copy_to(src, dst, ssem, rsem, device):
        return pltpu.make_async_remote_copy(
            src_ref=src, dst_ref=dst, send_sem=ssem, recv_sem=rsem,
            device_id=(group, device), device_id_type=MESH,
        )

    def outgoing(plan, u, d):
        send, got, ssem, rsem = plan
        return copy_to(send.at[u, d], got.at[u, me], ssem.at[u, d], rsem.at[u, me], d)

    def incoming(plan, u, s):
        send, got, ssem, rsem = plan
        return copy_to(send.at[u, s], got.at[u, s], ssem.at[u, s], rsem.at[u, s], s)

    left = (left_send, left_got, left_ssem, left_rsem)
    right = (right_send, right_got, right_ssem, right_rsem)
    back = (tri_send, tri_got, tri_ssem, tri_rsem)

    def send_chunk(plan, u):
        def narrow(d):
            for q in range(tiles):
                part = wide[q, pl.ds(pl.multiple_of(d * block, 16), block), :]
                plan[0][u, d, :, q * 128 : (q + 1) * 128] = part.astype(jnp.bfloat16)
        loop(0, n, narrow)
        loop(1, n, lambda t: outgoing(plan, u, peer(t)).start())
        plan[1][u, me] = plan[0][u, me]

    def receive_chunk(plan, u):
        loop(1, n, lambda t: incoming(plan, u, lax.rem(me + t, n)).wait_recv())

        def widen(s):
            for q in range(tiles):
                part = plan[1][u, s, :, q * 128 : (q + 1) * 128].astype(jnp.float32)
                wide[q, pl.ds(pl.multiple_of(s * block, 16), block), :] = part
        loop(0, n, widen)

    barrier = pltpu.get_barrier_semaphore()
    loop(1, n, lambda t: pl.semaphore_signal(
        barrier, inc=1, device_id=(group, lax.rem(me + t, n)), device_id_type=MESH))

    length = lax.fori_loop(0, residues, lambda i, total: total + mask_ref[i], jnp.int32(0))
    place = lax.broadcasted_iota(jnp.int32, (1, residues), 1)
    natural = lax.rem(place, n) * rows + place // n
    valid = jnp.where(natural < length, 1.0, 0.0)

    def pm(r):
        return valid * mask_ref[me * rows + r].astype(jnp.float32)

    tri_in_t[...] = to_t(tri_in_ref)

    def gated(r, place, first):
        proj = matmul(tri_in_t[first : first + 2 * width, :], xn[r])
        value = sigmoid(proj[width:]) * proj[:width] * pm(r)
        scatter_rows(wide, place, chunk, value)

    for u in range(chunks):
        at = pl.ds(u * chunk, chunk)
        pltpu.make_async_copy(pair_hbm.at[at], pair_ref.at[at], pair_sem.at[u]).wait()

        def right_row(t):
            r = u * chunk + t
            pair_t = jnp.concatenate(
                [pair_ref[r, pl.ds(rr, n, stride=rows), :] for rr in range(rows)], axis=0
            ).T
            pair1_ref[r] = pair_t
            xn[r] = norm_rows(pair_t).astype(jnp.bfloat16)
            gated(r, t, 2 * width)
        loop(0, chunk, right_row)
        if u == 0:
            pl.semaphore_wait(barrier, n - 1)
        send_chunk(right, u)
    for u in range(chunks):
        loop(0, chunk, lambda t: gated(u * chunk + t, t, 0))
        send_chunk(left, u)

    gate_t[...] = to_t(gate_ref)
    tri_out_t[...] = to_t(tri_out_ref)
    att_in_t[...] = to_t(att_in_ref)

    def gate_row(r):
        gating[r] = sigmoid(matmul(gate_t[...], xn[r])) * pm(r)
    loop(0, rows, gate_row)

    for u in range(chunks):
        receive_chunk(right, u)
        for c in range(per):
            for t in range(chunk):
                first = (u * chunk + t) * n
                part = gather_rows(wide, c * chunk + t, n, block)
                right_mat[c, first : first + n, :] = part.astype(jnp.bfloat16)
    for u in range(chunks):
        receive_chunk(left, u)
        for c in range(per):
            lefts = [gather_rows(wide, c * chunk + t, n, block) for t in range(chunk)]
            tri = lax.dot_general(
                jnp.concatenate(lefts, axis=0).astype(jnp.bfloat16), right_mat[c],
                (((1,), (1,)), ((), ())), preferred_element_type=jnp.float32,
            )
            for t in range(chunk):
                scatter_rows(wide, c * chunk + t, block, tri[t * n : (t + 1) * n])
        send_chunk(back, u)

    planes = n // PLANE
    low = lax.rem(me, PLANE)
    base = me - low
    twin_low = low - lax.rem(me, 2) + (1 - lax.rem(me, 2))
    twin = base + twin_low

    def put(u, b, ssem, device):
        return copy_to(bias_all.at[u, b], bias_all.at[u, b], ssem, bias_rsem.at[u, b], device)

    def along(step):
        return lax.rem(me + step * PLANE, n)

    def beside(step):
        return base + lax.rem(low + 2 * step, PLANE)

    def bias_first(u):
        for step in range(1, planes):
            put(u, me, z_ssem.at[u, step], along(step)).start()

    def bias_second(u):
        for z in range(planes):
            b = along(z)
            if z:
                put(u, b, z_ssem.at[u, z], me).wait_recv()
            for step in range(1, PLANE // 2):
                put(u, b, plane_ssem.at[u, z, step], beside(step)).start()
            put(u, b, core_ssem.at[u, z, 0], twin).start()

    def bias_third(u):
        for z in range(planes):
            for step in range(1, PLANE // 2):
                b = lax.rem(beside(step) + z * PLANE, n)
                put(u, b, plane_ssem.at[u, z, step], me).wait_recv()
                put(u, b, core_ssem.at[u, z, step], twin).start()

    def bias_last(u):
        for z in range(planes):
            for step in range(PLANE // 2):
                b = lax.rem(base + lax.rem(twin_low + 2 * step, PLANE) + z * PLANE, n)
                put(u, b, core_ssem.at[u, z, step], me).wait_recv()

    hide = jnp.where(natural < length, 0.0, -jnp.inf)

    def bias_finish(u):
        bias_last(u)
        tall = heads * chunk

        def widen(s):
            for q in range(tiles):
                part = bias_all[u, s, :, q * 128 : (q + 1) * 128].astype(jnp.float32)
                bias_rows[q, pl.ds(pl.multiple_of(s * tall, 16), tall), :] = part * LOG2E
        loop(0, n, widen)
        for h in range(heads):
            part = jnp.concatenate([gather_rows(bias_rows, h * chunk + t, n, tall) for t in range(chunk)], axis=0)
            bias_ref[h, :, u * chunk * n : (u + 1) * chunk * n] = (part + hide).T

    def bias_sent(u):
        for step in range(1, planes):
            put(u, me, z_ssem.at[u, step], along(step)).wait_send()
        for z in range(planes):
            for step in range(PLANE // 2):
                b = lax.rem(beside(step) + z * PLANE, n)
                put(u, b, core_ssem.at[u, z, step], twin).wait_send()
                if step:
                    put(u, along(z), plane_ssem.at[u, z, step], beside(step)).wait_send()

    scale = LOG2E / math.sqrt(hd // heads)

    def qkvg_row(r):
        qkvg = matmul(att_in_t[...], yn[r])
        qkv_ref[r, :hd, :] = (qkvg[:hd] * scale).astype(jnp.bfloat16)
        qkv_ref[r, hd:, :] = qkvg[hd : 3 * hd].astype(jnp.bfloat16)
        g_ref[r] = sigmoid(qkvg[3 * hd :]).astype(jnp.bfloat16)

    def store(u):
        at = pl.ds(u * chunk, chunk)
        pairs = ((pair1_ref, pair1_hbm), (qkv_ref, qkv_hbm), (g_ref, g_hbm))
        return [pltpu.make_async_copy(v.at[at], h.at[at], out_sem.at[u, k]) for k, (v, h) in enumerate(pairs)]

    for u in range(chunks):
        receive_chunk(back, u)

        def pair_row(t):
            r = u * chunk + t
            tnorm = norm_rows(gather_rows(wide, t, width, chunk)).astype(jnp.bfloat16)
            pair1 = pair1_ref[r] + gating[r] * matmul(tri_out_t[...], tnorm)
            pair1_ref[r] = pair1
            fresh = norm_rows(pair1).astype(jnp.bfloat16)
            yn[r] = fresh
            scatter_rows(bias_wide, t, chunk, matmul(bias_w_ref[...], fresh))
        loop(0, chunk, pair_row)
        bias_all[u, me] = all_rows(bias_wide).astype(jnp.bfloat16)
        bias_first(u)
        if u < chunks - 1:
            loop(u * chunk, (u + 1) * chunk, qkvg_row)
            for copy in store(u):
                copy.start()
        if u >= 1:
            bias_second(u - 1)
        if u >= 2:
            bias_third(u - 2)
    done = (chunks - 1) * chunk
    half = chunk // 2
    for u in range(chunks - 2):
        bias_finish(u)
    bias_second(chunks - 1)
    loop(done, done + half, qkvg_row)
    if chunks >= 2:
        bias_third(chunks - 2)
    bias_third(chunks - 1)
    loop(done + half, done + chunk, qkvg_row)
    for copy in store(chunks - 1):
        copy.start()
    for u in range(max(chunks - 2, 0), chunks):
        bias_finish(u)
    for u in range(chunks):
        bias_sent(u)
        for copy in store(u):
            copy.wait()
        for plan in (right, left, back):
            loop(1, n, lambda t: outgoing(plan, u, lax.rem(me + t, n)).wait_send())


def attention_kernel(n, bias_ref, live_ref, pair1_ref, qkv_ref, g_ref, att_out_ref, out_ref, out_t):
    heads, residues, _ = bias_ref.shape
    rows = residues // n
    hd = g_ref.shape[1]
    size = hd // heads

    @pl.when(pl.program_id(0) == 0)
    def _():
        out_t[...] = to_t(att_out_ref)

    ones = jnp.ones((16, residues), jnp.bfloat16)
    for i in range(out_ref.shape[0]):
        parts = []
        for h in range(heads):
            first = h * size
            query = qkv_ref[i, first : first + size, :]
            values = qkv_ref[i, 2 * hd + first : 2 * hd + first + size, :]
            keys = qkv_ref[i, hd + first : hd + first + size, :]
            scores = lax.dot_general(keys, query, (((0,), (0,)), ((), ())), preferred_element_type=jnp.float32)
            scores = scores + bias_ref[h]
            probs = jnp.exp2(scores - jnp.max(scores, axis=0, keepdims=True)).astype(jnp.bfloat16)
            mixed = matmul(jnp.concatenate([values, ones], axis=0), probs)
            gates = g_ref[i, first : first + size, :].astype(jnp.float32)
            parts.append((mixed[:size] * (1.0 / mixed[size : size + 1]) * gates).astype(jnp.bfloat16))
        out = matmul(out_t[...], jnp.concatenate(parts, axis=0))
        own = lax.axis_index("row") * rows + pl.program_id(0) * out_ref.shape[0] + i
        new = (pair1_ref[i] + live_ref[own].astype(jnp.float32) * out).T
        for r in range(rows):
            out_ref[i, pl.ds(r, n, stride=rows), :] = new[r * n : (r + 1) * n]


def chunk_rows(n, rows, width, heads):
    per = width // n
    for chunk in range(1, rows + 1):
        if rows % chunk == 0 and (chunk * n) % 128 == 0 and (per * chunk) % 16 == 0 and (heads * chunk) % 16 == 0:
            return chunk
    return 0


def fused(n, pair, mask, tri_in, tri_gate, tri_out, att_in, att_bias, att_out):
    rows, residues, width = pair.shape
    heads = att_bias.shape[1]
    hd = att_out.shape[0]
    per = width // n
    chunk = chunk_rows(n, rows, width, heads)
    chunks = rows // chunk
    tiles = residues // 128
    planes = n // PLANE
    bf, f32 = jnp.bfloat16, jnp.float32
    vmem = pl.BlockSpec(memory_space=pltpu.VMEM)
    smem = pl.BlockSpec(memory_space=pltpu.SMEM)
    hbm = pl.BlockSpec(memory_space=pl.ANY)
    dma = pltpu.SemaphoreType.DMA
    blocks = pltpu.VMEM((chunks, n, per * chunk, residues), bf)
    side = PLANE // 2
    many = 3 if rows % 3 == 0 else 1
    pair1, qkv, gates, bias = pl.pallas_call(
        functools.partial(triangle_kernel, n, chunk, heads),
        out_shape=(
            jax.ShapeDtypeStruct((rows, width, residues), f32),
            jax.ShapeDtypeStruct((rows, 3 * hd, residues), bf),
            jax.ShapeDtypeStruct((rows, hd, residues), bf),
            jax.ShapeDtypeStruct((heads, residues, residues), f32),
        ),
        in_specs=[hbm, smem] + [vmem] * 5,
        out_specs=(hbm, hbm, hbm, vmem),
        scratch_shapes=[
            pltpu.VMEM((rows, residues, width), f32),
            pltpu.VMEM((rows, width, residues), f32),
            pltpu.VMEM((rows, 3 * hd, residues), bf),
            pltpu.VMEM((rows, hd, residues), bf),
            dma((chunks,)),
            dma((chunks, 3)),
            pltpu.VMEM((tiles, width * chunk, 128), f32),
            pltpu.VMEM((tiles, heads * chunk, 128), f32),
            pltpu.VMEM((tiles, n * heads * chunk, 128), f32),
            pltpu.VMEM((per, residues, residues), bf),
            pltpu.VMEM((rows, width, residues), bf),
            pltpu.VMEM((rows, width, residues), bf),
            pltpu.VMEM((rows, width, residues), f32),
            pltpu.VMEM((4 * width, width), bf),
            pltpu.VMEM((width, width), bf),
            pltpu.VMEM((width, width), bf),
            pltpu.VMEM((4 * hd, width), bf),
        ] + [blocks] * 6 + [
            pltpu.VMEM((chunks, n, heads * chunk, residues), bf),
        ] + [dma((chunks, n))] * 6 + [
            dma((chunks, planes)), dma((chunks, planes, side)), dma((chunks, planes, side)), dma((chunks, n)),
        ],
        compiler_params=pltpu.CompilerParams(
            collective_id=0, has_side_effects=True, vmem_limit_bytes=60 * 2**20
        ),
    )(pair, mask, tri_in, tri_gate, tri_out, att_in, att_bias.T)

    def whole(shape):
        return pl.BlockSpec(shape, lambda i: (0,) * len(shape))

    def row(*shape):
        return pl.BlockSpec((many,) + shape, lambda i: (i, 0, 0))

    return pl.pallas_call(
        functools.partial(attention_kernel, n),
        grid=(rows // many,),
        out_shape=jax.ShapeDtypeStruct((rows, residues, width), f32),
        in_specs=[
            whole((heads, residues, residues)), smem,
            row(width, residues), row(3 * hd, residues), row(hd, residues), whole((hd, width)),
        ],
        out_specs=row(residues, width),
        scratch_shapes=[
            pltpu.VMEM((width, hd), bf),
        ],
        compiler_params=pltpu.CompilerParams(vmem_limit_bytes=60 * 2**20),
    )(bias, mask, pair1, qkv, gates, att_out)


def layer_norm(value):
    center = value - jnp.mean(value, axis=-1, keepdims=True)
    return center / jnp.sqrt(jnp.mean(center * center, axis=-1, keepdims=True) + 1e-05)


def per_device(pair, mask, tri_in, tri_gate, tri_out, att_in, att_bias, att_out):
    own_rows = pair.shape[0]
    residues = pair.shape[1]
    width = pair.shape[2]
    heads = att_bias.shape[1]
    head_size = att_out.shape[0] // heads
    valid = mask.astype(jnp.float32)
    start_row = lax.axis_index("row") * own_rows
    row_valid = lax.dynamic_slice_in_dim(valid, start_row, own_rows, 0)
    pair_mask = row_valid[:, None] * valid[None, :]
    normed = layer_norm(pair).astype(jnp.bfloat16)
    proj = jnp.einsum("rkc,cf->rkf", normed, tri_in, preferred_element_type=jnp.float32)
    left = (
        jax.nn.sigmoid(proj[..., width : 2 * width]) * proj[..., :width] * pair_mask[..., None]
    ).astype(jnp.bfloat16)
    right = (
        jax.nn.sigmoid(proj[..., 3 * width :])
        * proj[..., 2 * width : 3 * width]
        * pair_mask[..., None]
    ).astype(jnp.bfloat16)
    left_by_channel = jnp.transpose(left, (2, 0, 1))
    right_by_channel = jnp.transpose(right, (2, 0, 1))
    left_all, right_all = (
        lax.all_to_all(left_by_channel, "row", split_axis=0, concat_axis=1, tiled=True),
        lax.all_to_all(right_by_channel, "row", split_axis=0, concat_axis=1, tiled=True),
    )
    tri_channel = jnp.einsum(
        "cik,cjk->cij", left_all, right_all, preferred_element_type=jnp.float32
    )
    tri_rows = lax.all_to_all(
        tri_channel.astype(jnp.bfloat16), "row", split_axis=1, concat_axis=0, tiled=True
    ).astype(tri_channel.dtype)
    tri = jnp.transpose(tri_rows, (1, 2, 0))
    tnorm = layer_norm(tri).astype(jnp.bfloat16)
    update = jnp.einsum("rkc,cf->rkf", tnorm, tri_out, preferred_element_type=jnp.float32)
    gating = jax.nn.sigmoid(
        jnp.einsum("rkc,cf->rkf", normed, tri_gate, preferred_element_type=jnp.float32)
    )
    pair1 = pair + pair_mask[..., None] * gating * update
    ynorm = layer_norm(pair1).astype(jnp.bfloat16)
    qkvg = jnp.einsum("rkc,cf->rkf", ynorm, att_in, preferred_element_type=jnp.float32)
    qkvg = qkvg.reshape(own_rows, residues, 4, heads, head_size)
    query = qkvg[:, :, 0].astype(jnp.bfloat16)
    keys = qkvg[:, :, 1].astype(jnp.bfloat16)
    values = qkvg[:, :, 2].astype(jnp.bfloat16)
    gates = qkvg[:, :, 3]
    local_bias = jnp.einsum(
        "rkc,ch->hrk", ynorm, att_bias, preferred_element_type=jnp.float32
    ).astype(jnp.bfloat16)
    bias = lax.all_gather(local_bias, "row", axis=1, tiled=True)
    scores = jnp.einsum(
        "ijhd,ikhd->ihjk", query, keys, preferred_element_type=jnp.float32
    ) / jnp.sqrt(jnp.float32(head_size))
    scores = scores + bias.astype(jnp.float32)[None]
    scores = jnp.where(mask[None, None, None, :] > 0, scores, jnp.float32(-1000000000.0))
    probs = jax.nn.softmax(scores, axis=-1).astype(jnp.bfloat16)
    mixed = jnp.einsum("ihjk,ikhd->ijhd", probs, values, preferred_element_type=jnp.float32)
    att = (
        (jax.nn.sigmoid(gates) * mixed)
        .astype(jnp.bfloat16)
        .reshape(own_rows, residues, heads * head_size)
    )
    out = jnp.einsum("rkf,fc->rkc", att, att_out, preferred_element_type=jnp.float32)
    return pair1 + row_valid[:, None, None] * out


def solution(mesh):
    n = mesh.shape["row"]

    def per_shard(pair, mask, tri_in, tri_gate, tri_out, att_in, att_bias, att_out):
        rows, residues, width = pair.shape
        fits = (
            rows * n == residues and width % n == 0 and n % PLANE == 0 and n % 16 == 0 and residues % 128 == 0
            and chunk_rows(n, rows, width, att_bias.shape[1]) > 0
        )
        run = functools.partial(fused, n) if fits else per_device
        return run(pair, mask, tri_in, tri_gate, tri_out, att_in, att_bias, att_out)

    return jax.shard_map(
        per_shard,
        mesh=mesh,
        in_specs=(P(("groups", "row"), None, None), P("groups"), P(), P(), P(), P(), P(), P()),
        out_specs=P(("groups", "row"), None, None),
        check_vma=False,
    )
```
